128 devices in a mesh: dp: 16 (over y, x_hi, core), tensor: 8 (over z, x_lo).
Axes of the slice: x: 4 (x_hi: 2, x_lo: 2; x = x_hi * 2 + x_lo), y: 4, z: 4, core: 2. Of those that a mesh axis runs over, the one named last changes fastest.
Arguments:
- layer_input: bfloat16 [6144, 4096], P('dp', 'tensor'), may hold values from -6 to 6
- w_x: bfloat16 [4096, 4096], P(None, 'tensor'), may hold values from -0.09375 to 0.09375
- gate_in: bfloat16 [6144, 4096], P('dp', 'tensor'), may hold values from -6 to 6
- bc: bfloat16 [6144, 256], P('dp'), may hold values from -4 to 4
- dt_raw: float32 [64, 6144], P('tensor', 'dp'), may hold values from -2.5 to 4.5
- a_log: float32 [64], P('tensor'), may hold values from -6.2 to -2.8
- skip: float32 [64], P('tensor'), may hold values from 0.5 to 1.5
- gain: float32 [4096], P('tensor'), may hold values from 0.5 to 1.5
- doc_ids: int32 [6144], P('dp'), may hold values from 0 to 63, never falling along the last dimension, each value on 1 to 192 neighbouring positions
- d_out: bfloat16 [6144, 4096], P('dp', 'tensor'), may hold values from -6 to 6
- q_prev: float32 [32, 4096], P(None, 'tensor'), may hold values from -6 to 6
- error_in: float32 [65536, 4096], P('dp', 'tensor'), may hold values from -48 to 48
Outputs:
- d_input: bfloat16 [6144, 4096], P('dp', 'tensor')
- d_gate: bfloat16 [6144, 4096], P('dp', 'tensor')
- d_bc: float32 [6144, 256], P('dp')
- d_dt: float32 [64, 6144], P('tensor', 'dp')
- d_alog: float32 [64], P('tensor')
- d_skip: float32 [64], P('tensor')
- d_gain: float32 [4096], P('tensor')
- p_factor: float32 [256, 4096], P('tensor')
- right_factor_mean: float32 [32, 4096], P(None, 'tensor')
- error_out: float32 [65536, 4096], P('dp', 'tensor')
The draws below stay inside these ranges and needn't reach their ends.
Inputs may be any that keep to these rules, and one draw needn't show every extreme that they name: `doc_ids`: document numbers never fall along the tokens.
All inputs are finite; a program needn't handle non-finite values.
Results may differ from the reference program's by a relative error of at most 0.011.
Values may be sent and summed in bfloat16 or wider, within the bound.
A program may use at most 128 MiB of HBM per device.

```python
import math
import jax
import jax.numpy as jnp
import numpy as np
from jax import lax

D = 4096
HEADS = 64
HEADDIM = 64
STATE = 128
RANK = 32
TOK_DEV = 384
INNER = 4096
TOKEN_TOTAL = 6144
EROWS = 65536
PROWS = 256
N_DP = 16
N_TENSOR = 8


def draw_dt_raw(key, part):
    key = jax.random.fold_in(key, 11)
    random_base_key, spike_random_key = jax.random.split(key)
    baseline_values = jnp.clip(jax.random.normal(random_base_key, (HEADS, TOKEN_TOTAL), jnp.float32) * 0.6 - 0.5, -2.5, 1.5)
    spike_mask = jax.random.randint(spike_random_key, (1, TOKEN_TOTAL), 0, 97) == 0
    return (baseline_values + jnp.where(spike_mask, 3.0, 0.0)).astype(jnp.float32)


def levels(stream_key, shape, cuts, smallest, high):
    loudness, own = 1.0, jax.random.fold_in(stream_key, 6)
    for dim, blocks in cuts:
        steps = jnp.exp(jax.random.uniform(jax.random.fold_in(own, dim), (blocks,), jnp.float32, smallest / len(cuts), high / len(cuts)))
        loudness = loudness * jnp.repeat(steps, shape[dim] // blocks).reshape([-1 if axis == dim else 1 for axis in range(len(shape))])
    return loudness


def split_up(count, total, bound, slope):
    portions = [(1 << 20) // math.isqrt(grade ** slope) + 1 for grade in range(2, count + 1)]
    spare, given = total - bound - (count - 1), [1] * (count - 1)
    while spare > 0:
        free = [i for i in range(count - 1) if given[i] < bound]
        mass, budget = sum([portions[i] for i in free]), spare
        for i in free:
            addition = min(bound - given[i], max(1, budget * portions[i] // mass), spare)
            given[i] = given[i] + addition
            spare = spare - addition
    return np.array([bound] + given)


def ragged(stream_key, number_of, total, limit, lean):
    if number_of == 2:
        one = jax.random.randint(stream_key, (), max(1, total - limit), min(limit, total - 1) + 1)
        return jnp.stack([one, total - one])
    lengths = jnp.asarray(split_up(number_of, total, limit, lean), jnp.int32)
    pairs = (number_of - 1) // 2
    giver, taker = lengths[1:1 + 2 * pairs:2], lengths[2:2 + 2 * pairs:2]
    slack = jnp.minimum(giver - 1, limit - taker)
    shifted = jax.random.randint(jax.random.fold_in(stream_key, 1), (pairs,), 0, 1 << 20) % (slack + 1)
    lengths = lengths.at[1:1 + 2 * pairs:2].set(giver - shifted).at[2:2 + 2 * pairs:2].set(taker + shifted)
    return lengths[jax.random.permutation(jax.random.fold_in(stream_key, 2), number_of)]


def normal_values(rng, shape, scale, reach, shards=(), kind=jnp.bfloat16):
    array = scale * jax.random.normal(rng, shape, jnp.float32)
    if shards:
        array = array * levels(rng, shape, shards, -0.22, 0.18)
    return jnp.clip(array, -reach, reach).astype(kind)


def setup_inputs(seed: int = 0) -> dict:
    keys = jax.random.split(jax.random.key(seed), 13)
    return {
        "layer_input": normal_values(keys[0], (TOKEN_TOTAL, D), 1.0, 6.0, ((0, 16), (1, 8))),
        "w_x": normal_values(keys[1], (D, INNER), D ** -0.5, 0.09375, ((1, 8),)),
        "gate_in": normal_values(keys[2], (TOKEN_TOTAL, INNER), 1.0, 6.0, ((0, 16), (1, 8))),
        "bc": normal_values(keys[3], (TOKEN_TOTAL, 2 * STATE), 0.3, 4.0, ((0, 16),)),
        "dt_raw": draw_dt_raw(jax.random.fold_in(keys[12], 71), 0),
        "a_log": jnp.clip(-6.2 + 3.3999999 * jax.random.uniform(keys[5], (HEADS,), jnp.float32) ** levels(keys[5], (HEADS,), ((0, 8),), -0.2, 0.2), -6.2, -2.8),
        "skip": jnp.clip(0.5 + 1.0 * jax.random.uniform(keys[6], (HEADS,), jnp.float32) ** levels(keys[6], (HEADS,), ((0, 8),), -0.2, 0.2), 0.5, 1.5),
        "gain": jnp.clip(1.0 + 0.1 * jax.random.normal(keys[7], (INNER,), jnp.float32), 0.5, 1.5),
        "doc_ids": jnp.searchsorted(jnp.cumsum(ragged(keys[8], 4 * N_DP, TOKEN_TOTAL, TOK_DEV // 2, 0)), jnp.arange(TOKEN_TOTAL), side="right").astype(jnp.int32),
        "d_out": normal_values(keys[9], (TOKEN_TOTAL, INNER), 1.0, 6.0, ((0, 16), (1, 8))),
        "q_prev": normal_values(keys[10], (RANK, INNER), 1.0, 6.0, ((1, 8),), jnp.float32),
        "error_in": normal_values(keys[11], (EROWS, INNER), 8.0, 48.0, ((0, 16), (1, 8)), jnp.float32),
    }


EPSILON = 1e-05
HIGH = lax.Precision.HIGHEST

def head_mix(scores, keep_float, keep_mask, inner_head, step_head, decay_head, skip_head):
    step_rates = jnp.exp(decay_head) * step_head
    totals = jnp.cumsum(step_rates)
    decay_spans = totals[None, :] - totals[:, None]
    decays = jnp.exp(jnp.where(keep_mask, decay_spans, 0.0)) * keep_float
    weights = scores * decays * step_head[None, :]
    return jnp.dot(weights, inner_head, precision=HIGH) + skip_head * inner_head

def mix_heads(inner_heads, step_vals, decay_log, skip_gain, state_vals, doc_block):
    state_half = state_vals.shape[1] // 2
    scores = jnp.dot(state_vals[:, state_half:], state_vals[:, :state_half].T, precision=HIGH)
    places = jnp.arange(inner_heads.shape[1], dtype=jnp.int32)
    keep_mask = jnp.logical_and(doc_block[:, None] == doc_block[None, :], places[:, None] >= places[None, :])
    keep_float = keep_mask.astype(jnp.float32)

    def one_head(head_parts):
        return head_mix(scores, keep_float, keep_mask, head_parts[0], head_parts[1], head_parts[2], head_parts[3])
    return lax.map(jax.checkpoint(one_head), (inner_heads, step_vals, decay_log, skip_gain))

def worker(worker_index, layer_input, w_x, gate_in, bc, dt_raw, a_log, skip, gain, doc_ids, d_out, q_prev, error_in):
    first_token = (worker_index * TOK_DEV).astype(jnp.int32)
    token_rows = lax.dynamic_slice_in_dim(layer_input, first_token, TOK_DEV, 0)
    gate_block = lax.dynamic_slice_in_dim(gate_in, first_token, TOK_DEV, 0)
    state_block = lax.dynamic_slice_in_dim(bc, first_token, TOK_DEV, 0)
    raw_steps = lax.dynamic_slice_in_dim(dt_raw, first_token, TOK_DEV, 1)
    doc_block = lax.dynamic_slice_in_dim(doc_ids, first_token, TOK_DEV, 0)
    upstream = lax.dynamic_slice_in_dim(d_out, first_token, TOK_DEV, 0).astype(jnp.float32)
    error_block = lax.dynamic_slice_in_dim(error_in, (worker_index * D).astype(jnp.int32), D, 0)
    inner_vals = jnp.dot(token_rows.astype(jnp.float32), w_x.astype(jnp.float32), preferred_element_type=jnp.float32).astype(jnp.bfloat16)
    inner_heads = inner_vals.astype(jnp.float32).reshape(TOK_DEV, HEADS, HEADDIM).transpose(1, 0, 2)
    step_pos = jax.nn.softplus(raw_steps)

    def forward(heads_in, steps_in, decay_in, skip_in, states_in):
        return mix_heads(heads_in, steps_in, decay_in, skip_in, states_in, doc_block)
    mixed_heads, pullback = jax.vjp(forward, inner_heads, step_pos, a_log, skip, state_block.astype(jnp.float32))
    mixed = mixed_heads.transpose(1, 0, 2).reshape(TOK_DEV, INNER)
    gate_vals = gate_block.astype(jnp.float32)
    gate_sigmoid = jax.nn.sigmoid(gate_vals)
    silu_vals = gate_vals * gate_sigmoid
    gated = mixed * silu_vals
    row_scale = lax.rsqrt(lax.optimization_barrier(jnp.mean(gated * gated, axis=1)) + EPSILON)
    weighted = upstream * gain[None, :]
    inner_dot = lax.optimization_barrier(jnp.mean(gated * weighted, axis=1))
    grad_gated = row_scale[:, None] * weighted - gated * (row_scale ** 3 * inner_dot)[:, None]
    gain_part = lax.optimization_barrier(jnp.sum(upstream * gated * row_scale[:, None], axis=0))
    grad_gate = (grad_gated * mixed * gate_sigmoid * (1.0 + gate_vals * (1.0 - gate_sigmoid))).astype(jnp.bfloat16)
    grad_mixed = (grad_gated * silu_vals).reshape(TOK_DEV, HEADS, HEADDIM).transpose(1, 0, 2)
    grad_heads, grad_steps, grad_decay, grad_skip, grad_states = pullback(grad_mixed)
    grad_inner = grad_heads.transpose(1, 0, 2).reshape(TOK_DEV, INNER).astype(jnp.bfloat16)
    grad_rows = jnp.dot(grad_inner.astype(jnp.float32), w_x.T.astype(jnp.float32), preferred_element_type=jnp.float32).astype(jnp.bfloat16)
    grad_raw = grad_steps * jax.nn.sigmoid(raw_steps)
    merged = jnp.dot(token_rows.T.astype(jnp.float32), grad_inner.astype(jnp.float32), preferred_element_type=jnp.float32) + error_block
    inner_width = INNER // N_TENSOR
    factor = jnp.einsum('dki,rki->kdr', merged.reshape(D, N_TENSOR, inner_width), q_prev.reshape(RANK, N_TENSOR, inner_width), precision=HIGH)
    return (grad_rows, grad_gate, grad_states, grad_raw, grad_decay, grad_skip, gain_part, merged, factor)

def reference(layer_input, w_x, gate_in, bc, dt_raw, a_log, skip, gain, doc_ids, d_out, q_prev, error_in):

    def run_worker(worker_index):
        return worker(worker_index, layer_input, w_x, gate_in, bc, dt_raw, a_log, skip, gain, doc_ids, d_out, q_prev, error_in)
    results = lax.map(run_worker, jnp.arange(N_DP, dtype=jnp.int32))
    grad_rows, grad_gate, grad_states, grad_raw, grad_decay, grad_skip, gain_part, merged, factor = results
    d_input = grad_rows.reshape(TOKEN_TOTAL, D)
    d_gate = grad_gate.reshape(TOKEN_TOTAL, INNER)
    d_bc = grad_states.reshape(TOKEN_TOTAL, 2 * STATE)
    d_dt = grad_raw.transpose(1, 0, 2).reshape(HEADS, TOKEN_TOTAL)
    d_alog = lax.optimization_barrier(jnp.sum(grad_decay, axis=0))
    d_skip = lax.optimization_barrier(jnp.sum(grad_skip, axis=0))
    d_gain = lax.optimization_barrier(jnp.sum(gain_part, axis=0))
    factor_mean = lax.optimization_barrier(jnp.sum(factor, axis=0)) / N_DP
    gram_matrix = jnp.einsum('kdr,kds->krs', factor_mean, factor_mean, precision=HIGH)
    lower_factor = jnp.linalg.cholesky(gram_matrix)

    def solve_one(lower_block, right_side):
        return jax.scipy.linalg.solve_triangular(lower_block, right_side, lower=True)
    basis_t = jax.vmap(solve_one)(lower_factor, factor_mean.transpose(0, 2, 1))
    inner_width = INNER // N_TENSOR
    merged_blocks = merged.reshape(N_DP, D, N_TENSOR, inner_width)
    q_mean = jnp.einsum('krd,wdki->kri', basis_t, merged_blocks, precision=HIGH) / N_DP
    p_factor = basis_t.reshape(PROWS, D)
    right_factor_mean = q_mean.transpose(1, 0, 2).reshape(RANK, INNER)
    approx = jnp.einsum('krd,kri->dki', basis_t, q_mean, precision=HIGH)
    error_out = (merged_blocks - approx[None]).reshape(EROWS, INNER)
    return (d_input, d_gate, d_bc, d_dt, d_alog, d_skip, d_gain, p_factor, right_factor_mean, error_out)
```

```python
import jax
import jax.numpy as jnp
from jax import lax
from jax.experimental import pallas as pl
from jax.experimental.pallas import tpu as pltpu
from jax.sharding import PartitionSpec as P

EPSILON = 1e-05
HIGH = lax.Precision.HIGHEST
MESH = pl.DeviceIdType.MESH
F32 = jnp.float32
BF16 = jnp.bfloat16
T = 384
HALF = T // 2
HEADS = 8
CH = 512
NT = 8
NDP = 16
D = 4096
RANK = 32
BLK = 128
NB = T // BLK
LOW = -1e30
VMEM_LIMIT = 56 * 1024 * 1024


def dot_nn(a, b):
    return lax.dot_general(a, b, (((1,), (0,)), ((), ())), preferred_element_type=F32)


def dot_nt(a, b):
    return lax.dot_general(a, b, (((1,), (1,)), ((), ())), preferred_element_type=F32)


def split2(v):
    hi = v.astype(BF16)
    lo = (v - hi.astype(F32)).astype(BF16)
    return hi, lo


def split3(v):
    hi = v.astype(BF16)
    rest = v - hi.astype(F32)
    mid = rest.astype(BF16)
    lo = (rest - mid.astype(F32)).astype(BF16)
    return hi, mid, lo


def iota(shape, dim):
    return lax.broadcasted_iota(jnp.int32, shape, dim)


def to_column(row):
    return jnp.broadcast_to(row, (BLK, row.shape[1])).T


def head_rates(alog_ref):
    rows = iota((HEADS, T), 0)
    logs = jnp.zeros((HEADS, T), F32)
    for h in range(HEADS):
        logs = jnp.where(rows == h, alog_ref[h], logs)
    return jnp.exp(logs)


def softplus(v):
    return jnp.maximum(v, 0.0) + jnp.log1p(jnp.exp(-jnp.abs(v)))


def keep_bias(doc_ref, bias_ref, bias_t_ref):
    doc_row = doc_ref[...].astype(F32)
    doc_col = to_column(doc_row)
    for i in range(NB):
        for j in range(NB):
            rows = iota((BLK, BLK), 0) + i * BLK
            cols = iota((BLK, BLK), 1) + j * BLK
            same = doc_col[i * BLK : (i + 1) * BLK] == doc_row[:, j * BLK : (j + 1) * BLK]
            spot = (slice(i * BLK, (i + 1) * BLK), slice(j * BLK, (j + 1) * BLK))
            bias_ref[spot] = jnp.where(jnp.logical_and(same, rows >= cols), 0.0, LOW)
            if bias_t_ref is not None:
                bias_t_ref[spot] = jnp.where(jnp.logical_and(same, rows <= cols), 0.0, LOW)


def forward_kernel(
    x_ref, wx_hbm, e_hbm, gate_ref, dout_ref, bc_ref, dt_ref, alog_ref, skip_ref, gain_ref,
    doc_ref, q_ref,
    xall_hbm, eq_ref, inner_ref, dxb_ref, dy_ref, dgate_ref, stat_ref, cum_ref, rowp_ref,
    xall, wx, ebuf, w_mat, wt_mat, cum_col, rowp_col, bias, bias_t, scores, scores_t,
    acc, y_buf, sums, sums_in,
    x_send, x_recv, s_send, s_recv, wx_sem, e_sem, out_sem,
):
    me = lax.axis_index("tensor")
    z = me // 2
    xl = me % 2
    zp = ((z + 1) % 4) * 2 + xl
    zm = ((z + 3) % 4) * 2 + xl
    zo = ((z + 2) % 4) * 2 + xl
    xp = z * 2 + (1 - xl)

    barrier = pltpu.get_barrier_semaphore()
    for k in range(1, NT):
        pl.semaphore_signal(
            barrier, inc=1, device_id={"tensor": (me + k) % NT}, device_id_type=MESH
        )

    def wx_copy(b):
        rows = pl.ds(b * CH, CH)
        return pltpu.make_async_copy(wx_hbm.at[rows], wx.at[rows], wx_sem.at[b])

    def e_copy(b):
        return pltpu.make_async_copy(e_hbm.at[pl.ds(b * CH, CH)], ebuf.at[b % 2], e_sem.at[b % 2])

    e_copy(0).start()
    e_copy(1).start()
    for b in range(NT):
        wx_copy(b).start()

    xall[me] = x_ref[...]
    pl.semaphore_wait(barrier, NT - 1)

    def x_copy(way, to, src, half):
        part = xall.at[src, pl.ds(half * HALF, HALF)]
        return pltpu.make_async_remote_copy(
            src_ref=part,
            dst_ref=part,
            send_sem=x_send.at[way, src, half],
            recv_sem=x_recv.at[src, half],
            device_id={"tensor": to},
            device_id_type=MESH,
        )

    sent = []

    def send(way, to, src, half):
        copy = x_copy(way, to, src, half)
        copy.start()
        sent.append(copy)

    def arrive(src, half):
        x_copy(0, zp, src, half).wait_recv()

    for half in range(2):
        send(0, zp, me, half)
        send(1, zm, me, half)
        send(2, xp, me, half)

    step = softplus(dt_ref[...])
    rate = head_rates(alog_ref) * step
    upper = (iota((T, T), 0) <= iota((T, T), 1)).astype(F32)
    cum = jnp.dot(rate, upper, precision=HIGH, preferred_element_type=F32)
    cum_ref[...] = cum
    rowp_ref[...] = cum + jnp.log(step)
    keep_bias(doc_ref, bias, bias_t)
    b_part = bc_ref[:, :128]
    c_part = bc_ref[:, 128:]
    scores[...] = dot_nt(c_part, b_part)
    scores_t[...] = dot_nt(b_part, c_part)

    q_hi, q_lo = split2(q_ref[...])
    q_two = jnp.concatenate([q_hi, q_lo], axis=0)

    def e_block(b):
        e_copy(b).wait()
        e_hi, e_lo = split2(ebuf[b % 2])
        if b + 2 < NT:
            pass
        both = dot_nt(q_two, e_hi)
        eq_ref[:, b * CH : (b + 1) * CH] = both[:RANK] + both[RANK:] + dot_nt(q_hi, e_lo)
        if b + 2 < NT:
            e_copy(b + 2).start()

    for b in range(NT):
        e_block(b)

    arrive(zm, 0)
    send(0, zp, zm, 0)
    arrive(xp, 0)
    send(0, zp, xp, 0)
    send(1, zm, xp, 0)

    def weights(h, carry):
        cum_row = cum_ref[pl.ds(h, 1), :]
        rowp_row = rowp_ref[pl.ds(h, 1), :]
        col = to_column(cum_row)
        colp = to_column(rowp_row)
        for i in range(NB):
            here = slice(i * BLK, (i + 1) * BLK)
            for j in range(NB):
                there = slice(j * BLK, (j + 1) * BLK)
                if j <= i:
                    span = rowp_row[:, there] - col[here] + bias[here, there]
                    w_mat[h, here, there] = (scores[here, there] * jnp.exp(span)).astype(BF16)
                if j >= i:
                    span = colp[here] - cum_row[:, there] + bias_t[here, there]
                    wt_mat[h, here, there] = (scores_t[here, there] * jnp.exp(span)).astype(BF16)
        return carry

    lax.fori_loop(0, HEADS, weights, 0)

    arrive(zp, 1)
    send(1, zm, zp, 1)
    arrive(xp, 1)
    send(0, zp, xp, 1)
    send(1, zm, xp, 1)

    for b in range(NT):
        wx_copy(b).wait()
    arrive(zm, 1)
    arrive(zp, 0)

    def product(src):
        rows = pl.ds(pl.multiple_of(src * CH, CH), CH)
        return dot_nn(xall[src], wx[rows, :])

    acc[...] = product(me) + product(xp)
    acc[...] += product(zm) + product(zp)
    arrive(zo, 0)
    send(2, xp, zo, 0)
    arrive(zo, 1)
    send(2, xp, zo, 1)
    acc[...] += product(zo)
    xp_zp = ((z + 1) % 4) * 2 + (1 - xl)
    xp_zm = ((z + 3) % 4) * 2 + (1 - xl)
    xp_zo = ((z + 2) % 4) * 2 + (1 - xl)
    for other in (xp_zp, xp_zm, xp_zo):
        arrive(other, 0)
        arrive(other, 1)
        acc[...] += product(other)
    keep = pltpu.make_async_copy(xall, xall_hbm, out_sem)
    keep.start()
    inner_ref[...] = acc[...].astype(BF16)

    low_lanes = iota((1, BLK), 1) < 64

    def pair_lanes(p):
        return pl.ds(pl.multiple_of(p * BLK, BLK), BLK)

    def pair_skip(p):
        return jnp.where(low_lanes, skip_ref[2 * p], skip_ref[2 * p + 1])

    def gate_parts(lanes):
        gate = gate_ref[:, lanes].astype(F32)
        sig = 1.0 / (1.0 + jnp.exp(-gate))
        return gate, sig, gate * sig

    def mix(p, carry):
        square, product_sum = carry
        lanes = pair_lanes(p)
        x_pair = inner_ref[:, lanes]
        for i in range(NB):
            here = slice(i * BLK, (i + 1) * BLK)
            width = (i + 1) * BLK
            first = dot_nn(w_mat[2 * p, here, :width], x_pair[:width])
            second = dot_nn(w_mat[2 * p + 1, here, :width], x_pair[:width])
            y_buf[here, lanes] = jnp.where(low_lanes, first, second) + pair_skip(
                p
            ) * x_pair[here].astype(F32)
        gate, sig, silu = gate_parts(lanes)
        g = y_buf[:, lanes] * silu
        weighted = dout_ref[:, lanes].astype(F32) * gain_ref[:, lanes]
        return square + g * g, product_sum + g * weighted

    zero = jnp.zeros((T, BLK), F32)
    square, product_sum = lax.fori_loop(0, HEADS // 2, mix, (zero, zero))
    sums[0:1, :] = jnp.sum(square.T, axis=0, keepdims=True)
    sums[1:2, :] = jnp.sum(product_sum.T, axis=0, keepdims=True)
    sums[2:8, :] = jnp.zeros((6, T), F32)

    def s_copy(k):
        return pltpu.make_async_remote_copy(
            src_ref=sums,
            dst_ref=sums_in.at[k],
            send_sem=s_send.at[k],
            recv_sem=s_recv.at[k],
            device_id={"tensor": (me + k) % NT},
            device_id_type=MESH,
        )

    for k in range(1, NT):
        s_copy(k).start()
    total = sums[...]
    for k in range(1, NT):
        s_copy(k).wait_recv()
        total = total + sums_in[k]
    r_row = lax.rsqrt(total[0:1] / D + EPSILON)
    r_col = to_column(r_row)
    m_col = to_column(r_row * r_row * r_row * (total[1:2] / D))

    def back(p, carry):
        lanes = pair_lanes(p)
        gate, sig, silu = gate_parts(lanes)
        y = y_buf[:, lanes]
        g = y * silu
        up = dout_ref[:, lanes].astype(F32)
        dg = r_col * (up * gain_ref[:, lanes]) - g * m_col
        dgate_ref[:, lanes] = (dg * y * sig * (1.0 + gate * (1.0 - sig))).astype(BF16)
        dy = dg * silu
        dy_low = dy.astype(BF16)
        dy_ref[:, lanes] = dy_low
        stat_ref[pl.ds(p, 1), :] = jnp.sum(up * g * r_col, axis=0, keepdims=True)
        stat_ref[pl.ds(4 + p, 1), :] = jnp.sum(
            dy * inner_ref[:, lanes].astype(F32), axis=0, keepdims=True
        )
        for i in range(NB):
            here = slice(i * BLK, (i + 1) * BLK)
            first = dot_nn(wt_mat[2 * p, here, i * BLK :], dy_low[i * BLK :])
            second = dot_nn(wt_mat[2 * p + 1, here, i * BLK :], dy_low[i * BLK :])
            dxb_ref[here, lanes] = (
                jnp.where(low_lanes, first, second) + pair_skip(p) * dy[here]
            ).astype(BF16)
        return carry

    lax.fori_loop(0, HEADS // 2, back, 0)
    for copy in sent:
        copy.wait_send()
    for k in range(1, NT):
        s_copy(k).wait_send()
    keep.wait()


def factor_kernel(
    xall_hbm, e_hbm, wx_hbm, eq_ref, dxb_ref, dy_ref, inner_ref, q_ref, bc_ref, cum_ref, rowp_ref,
    dt_ref, doc_ref, alog_ref, stat_ref,
    ph_ref, qm_ref, dinp_ref, dbc_ref, ddt_ref, pay_ref,
    xall, e_all, wx, p_send, p_in, p_own, p_full, d_out, d_in, d_own, b_out, b_in, b_sum,
    bias, scores, d_scores, row_sum, col_sum, pay, pay_in, q_out, q_in, q_own, q_full,
    load_sem, e_sem, ps_sem, pr_sem, gs_sem, gr_sem, ds_sem, dr_sem, bs_sem, br_sem, cs_sem, cr_sem,
    ys_sem, yr_sem, qs_sem, qr_sem, hs_sem, hr_sem,
):
    w = lax.axis_index("dp")
    me = lax.axis_index("tensor")
    barrier = pltpu.get_barrier_semaphore()

    def greet_workers(k, carry):
        pl.semaphore_signal(barrier, inc=1, device_id={"dp": (w + k) % NDP}, device_id_type=MESH)
        return carry

    def greet_shards(k, carry):
        pl.semaphore_signal(barrier, inc=1, device_id={"tensor": (me + k) % NT}, device_id_type=MESH)
        return carry

    lax.fori_loop(1, NDP, greet_workers, 0)
    lax.fori_loop(1, NT, greet_shards, 0)
    x_load = pltpu.make_async_copy(xall_hbm, xall, load_sem.at[0])
    x_load.start()
    wx_load = pltpu.make_async_copy(wx_hbm, wx, load_sem.at[1])
    wx_load.start()
    e_load = pltpu.make_async_copy(e_hbm, e_all, e_sem)
    e_load.start()

    def remote(src, dst, send_sem, recv_sem, axis, to):
        return pltpu.make_async_remote_copy(
            src_ref=src, dst_ref=dst, send_sem=send_sem, recv_sem=recv_sem,
            device_id={axis: to}, device_id_type=MESH,
        )

    def loop(count, body):
        def step(k, carry):
            body(k)
            return carry
        lax.fori_loop(1, count, step, 0)

    dxb = dxb_ref[...]
    q3 = jnp.concatenate(split3(q_ref[...]), axis=0)
    z3 = dot_nt(q3, dxb)
    z_sum = z3[:RANK] + z3[RANK : 2 * RANK] + z3[2 * RANK :]
    z_three = jnp.concatenate(split3(z_sum), axis=0)
    x_load.wait()
    for s in range(NT):
        part = dot_nn(z_three, xall[s])
        part = part[:RANK] + part[RANK : 2 * RANK] + part[2 * RANK :]
        part = part + eq_ref[:, s * CH : (s + 1) * CH]
        p_send[2 * s] = part[:, :256]
        p_send[2 * s + 1] = part[:, 256:]
    pl.semaphore_wait(barrier, NDP - 1 + NT - 1)

    def p_copy(k):
        to = (w + k) % NDP
        return remote(p_send.at[to], p_in.at[k], ps_sem.at[k], pr_sem.at[k], "dp", to)

    loop(NDP, lambda k: p_copy(k).start())

    wx_load.wait()

    def d_copy(k):
        to = (me + k) % NT
        return remote(d_out.at[k], d_in.at[k], ds_sem.at[k], dr_sem.at[k], "tensor", to)

    def input_part(s):
        rows = pl.ds(pl.multiple_of(s * CH, CH), CH)
        return dot_nt(dxb, wx[rows, :])

    def send_input(k):
        d_out[k] = input_part((me + k) % NT).astype(BF16)
        d_copy(k).start()

    loop(NT, send_input)
    d_own[...] = input_part(me)

    keep_bias(doc_ref, bias, None)
    b_part = bc_ref[:, :128]
    c_part = bc_ref[:, 128:]
    scores[...] = dot_nt(c_part, b_part)
    d_scores[...] = jnp.zeros((T, T), F32)
    low_lanes = iota((1, BLK), 1) < 64

    def head_back(p, carry):
        lanes = pl.ds(pl.multiple_of(p * BLK, BLK), BLK)
        x_pair = inner_ref[:, lanes]
        dy_pair = dy_ref[:, lanes]
        for side in range(2):
            h = 2 * p + side
            mine = low_lanes if side == 0 else jnp.logical_not(low_lanes)
            x_mine = jnp.where(mine, x_pair, jnp.zeros_like(x_pair))
            rowp_row = rowp_ref[pl.ds(h, 1), :]
            col = to_column(cum_ref[pl.ds(h, 1), :])
            downs = [jnp.zeros((1, BLK), F32) for _ in range(NB)]
            acrosses = []
            for i in range(NB):
                here = slice(i * BLK, (i + 1) * BLK)
                width = (i + 1) * BLK
                d_weight = dot_nt(dy_pair[here], x_mine[:width])
                across = jnp.zeros((BLK, BLK), F32)
                for j in range(i + 1):
                    there = slice(j * BLK, (j + 1) * BLK)
                    span = rowp_row[:, there] - col[here] + bias[here, there]
                    d_score = d_weight[:, there] * jnp.exp(span)
                    d_scores[here, there] += d_score
                    both = d_score * scores[here, there]
                    downs[j] = downs[j] + jnp.sum(both, axis=0, keepdims=True)
                    across = across + both
                acrosses.append(jnp.sum(across.T, axis=0, keepdims=True))
            col_sum[pl.ds(h, 1), :] = jnp.concatenate(downs, axis=1)
            row_sum[pl.ds(h, 1), :] = jnp.concatenate(acrosses, axis=1)
        return carry

    lax.fori_loop(0, HEADS // 2, head_back, 0)
    ds_t = d_scores[...].T.astype(BF16)
    ds_low = d_scores[...].astype(BF16)
    db = dot_nn(ds_t, c_part)
    dc = dot_nn(ds_low, b_part)
    rows_each = T // NT
    for s in range(NT):
        b_out[s, :, :128] = db[s * rows_each : (s + 1) * rows_each]
        b_out[s, :, 128:] = dc[s * rows_each : (s + 1) * rows_each]

    def b_copy(k):
        to = (me + k) % NT
        return remote(b_out.at[to], b_in.at[k], bs_sem.at[k], br_sem.at[k], "tensor", to)

    loop(NT, lambda k: b_copy(k).start())

    lower = (iota((T, T), 0) >= iota((T, T), 1)).astype(F32)
    columns = col_sum[...]
    d_rate = jnp.dot(
        columns - row_sum[...], lower, precision=HIGH, preferred_element_type=F32
    )
    raw = dt_ref[...]
    step = softplus(raw)
    decay = head_rates(alog_ref)
    d_step = columns / step + decay * d_rate
    ddt_ref[...] = d_step / (1.0 + jnp.exp(-raw))
    pay[0:8, :] = stat_ref[...]
    pay[8:16, :] = jnp.broadcast_to(
        jnp.sum(d_rate * decay * step, axis=1, keepdims=True), (HEADS, BLK)
    )

    def pay_copy(k):
        return remote(pay, pay_in.at[k], ys_sem.at[k], yr_sem.at[k], "dp", (w + k) % NDP)

    loop(NDP, lambda k: pay_copy(k).start())

    def p_add(k, total):
        p_copy(k).wait_recv()
        return total + p_in[k]

    p_sum = lax.fori_loop(1, NDP, p_add, p_send[w]) / NDP
    p_own[...] = p_sum
    p_full[w] = p_sum

    def g_copy(k, slot):
        return remote(p_own, p_full.at[slot], gs_sem.at[k], gr_sem.at[k], "dp", (w + k) % NDP)

    loop(NDP, lambda k: g_copy(k, w).start())

    def b_add(k, total):
        b_copy(k).wait_recv()
        return total + b_in[k]

    b_total = lax.fori_loop(1, NT, b_add, b_out[me])
    b_sum[...] = b_total
    my_rows = pl.ds(pl.multiple_of(me * rows_each, 8), rows_each)
    dbc_ref[my_rows, :] = b_total

    def c_copy(k, slot):
        rows = pl.ds(pl.multiple_of(slot * rows_each, 8), rows_each)
        return remote(b_sum, dbc_ref.at[rows], cs_sem.at[k], cr_sem.at[k], "tensor", (me + k) % NT)

    loop(NT, lambda k: c_copy(k, me).start())

    loop(NDP, lambda k: g_copy(k, (w + NDP - k) % NDP).wait_recv())

    def gram_add(c, total):
        three = jnp.concatenate(split3(p_full[c]), axis=0)
        return total + dot_nt(three, three)

    g9 = lax.fori_loop(0, NDP, gram_add, jnp.zeros((3 * RANK, 3 * RANK), F32))
    g3 = g9[:RANK] + g9[RANK : 2 * RANK] + g9[2 * RANK :]
    gram = g3[:, :RANK] + g3[:, RANK : 2 * RANK] + g3[:, 2 * RANK :]
    eye = (iota((RANK, RANK), 0) == iota((RANK, RANK), 1)).astype(F32)
    table = jnp.concatenate([eye, gram], axis=1)
    places = iota((RANK, 2 * RANK), 0)
    for j in range(RANK - 1):
        column = table[:, RANK + j : RANK + j + 1]
        row = table[j : j + 1, :]
        pivot = table[j : j + 1, RANK + j : RANK + j + 1]
        table = table - jnp.where(places > j, column * (row / pivot), 0.0)
    pivots = jnp.sum(jnp.where(eye > 0.0, table[:, RANK:], 0.0), axis=1, keepdims=True)
    inverse = table[:, :RANK] * lax.rsqrt(pivots)

    for c in range(NDP):
        ph_ref[:, c * 256 : (c + 1) * 256] = jnp.dot(
            inverse, p_full[c], precision=HIGH, preferred_element_type=F32
        )

    e_load.wait()

    def q_part(s, carry):
        rotated, total = carry
        lanes = pl.ds(pl.multiple_of(s * CH, CH), CH)
        hi, lo = split2(ph_ref[:, lanes])
        two = jnp.concatenate([hi, lo], axis=0)
        rotated = rotated + dot_nt(two, xall[s])
        e_hi, e_lo = split2(e_all[lanes, :])
        both = dot_nn(two, e_hi)
        return rotated, total + both[:RANK] + both[RANK:] + dot_nn(hi, e_lo)

    rotated, total = lax.fori_loop(
        0, NT, q_part, (jnp.zeros((2 * RANK, T), F32), jnp.zeros((RANK, CH), F32))
    )
    two = jnp.concatenate(split2(rotated[:RANK] + rotated[RANK:]), axis=0)
    both = dot_nn(two, dxb)
    q_local = total + both[:RANK] + both[RANK:]
    for c in range(NDP):
        a, b = c // 4, c % 4
        q_out[c] = q_local[a * 8 : (a + 1) * 8, b * BLK : (b + 1) * BLK]

    def q_copy(k):
        to = (w + k) % NDP
        return remote(q_out.at[to], q_in.at[k], qs_sem.at[k], qr_sem.at[k], "dp", to)

    loop(NDP, lambda k: q_copy(k).start())

    def pay_add(k, total):
        pay_copy(k).wait_recv()
        return total + pay_in[k]

    pay_ref[...] = lax.fori_loop(1, NDP, pay_add, pay[...])

    def q_add(k, total):
        q_copy(k).wait_recv()
        return total + q_in[k]

    q_sum = lax.fori_loop(1, NDP, q_add, q_out[w]) / NDP
    q_own[...] = q_sum
    q_full[w] = q_sum

    def h_copy(k, slot):
        return remote(q_own, q_full.at[slot], hs_sem.at[k], hr_sem.at[k], "dp", (w + k) % NDP)

    loop(NDP, lambda k: h_copy(k, w).start())

    def d_add(k):
        d_copy(k).wait_recv()
        d_own[...] += d_in[k].astype(F32)

    loop(NT, d_add)
    dinp_ref[...] = d_own[...].astype(BF16)

    loop(NT, lambda k: c_copy(k, (me + NT - k) % NT).wait_recv())
    loop(NDP, lambda k: h_copy(k, (w + NDP - k) % NDP).wait_recv())
    for c in range(NDP):
        a, b = c // 4, c % 4
        qm_ref[a * 8 : (a + 1) * 8, b * BLK : (b + 1) * BLK] = q_full[c]

    def finish_workers(k):
        p_copy(k).wait_send()
        g_copy(k, w).wait_send()
        pay_copy(k).wait_send()
        q_copy(k).wait_send()
        h_copy(k, w).wait_send()

    def finish_shards(k):
        d_copy(k).wait_send()
        b_copy(k).wait_send()
        c_copy(k, me).wait_send()

    loop(NDP, finish_workers)
    loop(NT, finish_shards)


def error_kernel(
    e_ref, x_ref, dxb_ref, ph_ref, qm_ref, dinp_ref, dbc_ref, ddt_ref, dgate_ref,
    out_ref, ph_out, qm_out, dinp_out, dbc_out, ddt_out, dgate_out, right
):
    b = pl.program_id(0)

    @pl.when(b == 0)
    def _():
        q_hi, q_lo = split2(-qm_ref[...])
        right[:T] = dxb_ref[...]
        right[T : T + RANK] = q_hi
        right[T + RANK : T + 2 * RANK] = q_lo
        right[T + 2 * RANK :] = q_hi
        qm_out[...] = qm_ref[...]
        dinp_out[...] = dinp_ref[...]
        dbc_out[...] = dbc_ref[...]
        ddt_out[...] = ddt_ref[...]
        dgate_out[...] = dgate_ref[...]

    ph = ph_ref[...]
    ph_out[...] = ph
    hi, lo = split2(ph)
    left = jnp.concatenate([x_ref[0], hi, hi, lo], axis=0)
    out_ref[...] = e_ref[...] + lax.dot_general(
        left, right[...], (((0,), (0,)), ((), ())), preferred_element_type=F32
    )


def vmem():
    return pl.BlockSpec(memory_space=pltpu.VMEM)


def smem():
    return pl.BlockSpec(memory_space=pltpu.SMEM)


def hbm():
    return pl.BlockSpec(memory_space=pl.ANY)


def shape(dims, dtype=F32):
    return jax.ShapeDtypeStruct(dims, dtype)


DMA = pltpu.SemaphoreType.DMA


def shards(
    layer_input, w_x, gate_in, bc, dt_raw, a_log, skip, gain, doc_ids, d_out, q_prev, error_in
):
    doc_row = doc_ids.reshape(1, T)
    gain_row = gain.reshape(1, CH)
    xall, eq, inner, dxb, dy, d_gate, stat, cum, rowp = pl.pallas_call(
        forward_kernel,
        name="forward",
        out_shape=(
            shape((NT, T, CH), BF16), shape((RANK, D)), shape((T, CH), BF16), shape((T, CH), BF16),
            shape((T, CH), BF16), shape((T, CH), BF16), shape((8, BLK)), shape((HEADS, T)),
            shape((HEADS, T)),
        ),
        in_specs=[
            vmem(), hbm(), hbm(), vmem(), vmem(), vmem(), vmem(), smem(), smem(), vmem(), vmem(),
            vmem(),
        ],
        out_specs=(hbm(),) + (vmem(),) * 8,
        scratch_shapes=[
            pltpu.VMEM((NT, T, CH), BF16),
            pltpu.VMEM((D, CH), BF16),
            pltpu.VMEM((2, CH, CH), F32),
            pltpu.VMEM((HEADS, T, T), BF16),
            pltpu.VMEM((HEADS, T, T), BF16),
            pltpu.VMEM((8, BLK), F32),
            pltpu.VMEM((8, BLK), F32),
            pltpu.VMEM((T, T), F32),
            pltpu.VMEM((T, T), F32),
            pltpu.VMEM((T, T), F32),
            pltpu.VMEM((T, T), F32),
            pltpu.VMEM((T, CH), F32),
            pltpu.VMEM((T, CH), F32),
            pltpu.VMEM((8, T), F32),
            pltpu.VMEM((NT, 8, T), F32),
            DMA((3, NT, 2)),
            DMA((NT, 2)),
            DMA((NT,)),
            DMA((NT,)),
            DMA((NT,)),
            DMA((2,)),
            DMA,
        ],
        compiler_params=pltpu.CompilerParams(
            collective_id=0, has_side_effects=True, vmem_limit_bytes=VMEM_LIMIT
        ),
    )(
        layer_input, w_x, error_in, gate_in, d_out, bc, dt_raw, a_log, skip, gain_row, doc_row,
        q_prev,
    )
    ph, qm, d_input, d_bc, d_dt, pay = pl.pallas_call(
        factor_kernel,
        name="factor",
        out_shape=(
            shape((RANK, D)), shape((RANK, CH)), shape((T, CH), BF16), shape((T, 256)),
            shape((HEADS, T)), shape((16, BLK)),
        ),
        in_specs=[hbm()] * 3 + [vmem()] * 10 + [smem(), vmem()],
        out_specs=(vmem(),) * 6,
        scratch_shapes=[
            pltpu.VMEM((NT, T, CH), BF16),
            pltpu.VMEM((D, CH), F32),
            pltpu.VMEM((D, CH), BF16),
            pltpu.VMEM((NDP, RANK, 256), F32),
            pltpu.VMEM((NDP, RANK, 256), F32),
            pltpu.VMEM((RANK, 256), F32),
            pltpu.VMEM((NDP, RANK, 256), F32),
            pltpu.VMEM((NT, T, CH), BF16),
            pltpu.VMEM((NT, T, CH), BF16),
            pltpu.VMEM((T, CH), F32),
            pltpu.VMEM((NT, T // NT, 256), F32),
            pltpu.VMEM((NT, T // NT, 256), F32),
            pltpu.VMEM((T // NT, 256), F32),
            pltpu.VMEM((T, T), F32),
            pltpu.VMEM((T, T), F32),
            pltpu.VMEM((T, T), F32),
            pltpu.VMEM((HEADS, T), F32),
            pltpu.VMEM((HEADS, T), F32),
            pltpu.VMEM((16, BLK), F32),
            pltpu.VMEM((NDP, 16, BLK), F32),
            pltpu.VMEM((NDP, 8, BLK), F32),
            pltpu.VMEM((NDP, 8, BLK), F32),
            pltpu.VMEM((8, BLK), F32),
            pltpu.VMEM((NDP, 8, BLK), F32),
            DMA((2,)),
            DMA,
            DMA((NDP,)), DMA((NDP,)), DMA((NDP,)), DMA((NDP,)),
            DMA((NT,)), DMA((NT,)), DMA((NT,)), DMA((NT,)), DMA((NT,)), DMA((NT,)),
            DMA((NDP,)), DMA((NDP,)), DMA((NDP,)), DMA((NDP,)), DMA((NDP,)), DMA((NDP,)),
        ],
        compiler_params=pltpu.CompilerParams(
            collective_id=1, has_side_effects=True, vmem_limit_bytes=VMEM_LIMIT
        ),
    )(
        xall, error_in, w_x, eq, dxb, dy, inner, q_prev, bc, cum, rowp, dt_raw, doc_row, a_log,
        stat,
    )

    def whole(dims):
        return pl.BlockSpec(dims, lambda b: (0,) * len(dims))

    error_out, p_factor, right_mean, d_input, d_bc, d_dt, d_gate = pl.pallas_call(
        error_kernel,
        name="error",
        grid=(NT,),
        out_shape=(
            shape((D, CH)), shape((RANK, D)), shape((RANK, CH)), shape((T, CH), BF16),
            shape((T, 256)), shape((HEADS, T)), shape((T, CH), BF16),
        ),
        in_specs=[
            pl.BlockSpec((CH, CH), lambda b: (b, 0)),
            pl.BlockSpec((1, T, CH), lambda b: (b, 0, 0)),
            whole((T, CH)),
            pl.BlockSpec((RANK, CH), lambda b: (0, b)),
            whole((RANK, CH)),
            whole((T, CH)),
            whole((T, 256)),
            whole((HEADS, T)),
            whole((T, CH)),
        ],
        out_specs=(
            pl.BlockSpec((CH, CH), lambda b: (b, 0)),
            pl.BlockSpec((RANK, CH), lambda b: (0, b)),
            whole((RANK, CH)),
            whole((T, CH)),
            whole((T, 256)),
            whole((HEADS, T)),
            whole((T, CH)),
        ),
        scratch_shapes=[pltpu.VMEM((T + 3 * RANK, CH), BF16)],
        compiler_params=pltpu.CompilerParams(vmem_limit_bytes=VMEM_LIMIT),
    )(error_in, xall, dxb, ph, qm, d_input, d_bc, d_dt, d_gate)
    d_gain = pay[0:4].reshape(CH)
    d_skip = jnp.sum(pay[4:8].reshape(HEADS, 64), axis=1)
    d_alog = pay[8:16, 0]
    return (
        d_input, d_gate, d_bc, d_dt, d_alog, d_skip, d_gain, p_factor, right_mean, error_out,
    )


def solution(mesh):
    return jax.shard_map(
        shards,
        mesh=mesh,
        in_specs=(
            P("dp", "tensor"),
            P(None, "tensor"),
            P("dp", "tensor"),
            P("dp", None),
            P("tensor", "dp"),
            P("tensor"),
            P("tensor"),
            P("tensor"),
            P("dp"),
            P("dp", "tensor"),
            P(None, "tensor"),
            P("dp", "tensor"),
        ),
        out_specs=(
            P("dp", "tensor"),
            P("dp", "tensor"),
            P("dp", None),
            P("tensor", "dp"),
            P("tensor"),
            P("tensor"),
            P("tensor"),
            P("tensor", None),
            P(None, "tensor"),
            P("dp", "tensor"),
        ),
        check_vma=False,
    )
```

```python
import jax
import jax.numpy as jnp
from jax import lax
from jax.experimental import pallas as pl
from jax.experimental.pallas import tpu as pltpu
from jax.sharding import PartitionSpec as P

EPSILON = 1e-05
HIGH = lax.Precision.HIGHEST
MESH = pl.DeviceIdType.MESH
F32 = jnp.float32
BF16 = jnp.bfloat16
T = 384
HALF = T // 2
HEADS = 8
CH = 512
NT = 8
NDP = 16
D = 4096
RANK = 32
BLK = 128
NB = T // BLK
LOW = -1e30
VMEM_LIMIT = 56 * 1024 * 1024


def dot_nn(a, b):
    return lax.dot_general(a, b, (((1,), (0,)), ((), ())), preferred_element_type=F32)


def dot_nt(a, b):
    return lax.dot_general(a, b, (((1,), (1,)), ((), ())), preferred_element_type=F32)


def split2(v):
    hi = v.astype(BF16)
    lo = (v - hi.astype(F32)).astype(BF16)
    return hi, lo


def split3(v):
    hi = v.astype(BF16)
    rest = v - hi.astype(F32)
    mid = rest.astype(BF16)
    lo = (rest - mid.astype(F32)).astype(BF16)
    return hi, mid, lo


def iota(shape, dim):
    return lax.broadcasted_iota(jnp.int32, shape, dim)


def to_column(row):
    return jnp.broadcast_to(row, (BLK, row.shape[1])).T


def head_rates(alog_ref):
    rows = iota((HEADS, T), 0)
    logs = jnp.zeros((HEADS, T), F32)
    for h in range(HEADS):
        logs = jnp.where(rows == h, alog_ref[h], logs)
    return jnp.exp(logs)


def softplus(v):
    return jnp.maximum(v, 0.0) + jnp.log1p(jnp.exp(-jnp.abs(v)))


def keep_bias(doc_ref, bias_ref, bias_t_ref):
    doc_row = doc_ref[...].astype(F32).reshape(1, T)
    doc_col = to_column(doc_row)
    for i in range(NB):
        for j in range(NB):
            rows = iota((BLK, BLK), 0) + i * BLK
            cols = iota((BLK, BLK), 1) + j * BLK
            same = doc_col[i * BLK : (i + 1) * BLK] == doc_row[:, j * BLK : (j + 1) * BLK]
            spot = (slice(i * BLK, (i + 1) * BLK), slice(j * BLK, (j + 1) * BLK))
            bias_ref[spot] = jnp.where(jnp.logical_and(same, rows >= cols), 0.0, LOW)
            if bias_t_ref is not None:
                bias_t_ref[spot] = jnp.where(jnp.logical_and(same, rows <= cols), 0.0, LOW)


def main_kernel(
    x_ref, wx_hbm, e_hbm, gate_ref, dout_ref, bc_ref, dt_ref, alog_ref, skip_ref, gain_ref,
    doc_ref, q_ref,
    m_hbm, ph_ref, qm_ref, dinp_ref, dbc_ref, ddt_ref, dgate_ref, pay_ref,
    xall, wx, e_all, eq_ref, w_mat, wt_mat, bias, bias_t, scores, scores_t, d_scores,
    cum_ref, rowp_ref, row_sum, col_sum, acc, y_buf, inner_ref, dxb_ref, dy_ref, sums, sums_in,
    p_send, core_in, p_mid, y_in, p_low, x_in, p_full,
    dx_out, part_out, opp_out, near_out, near_hold, dx_in, part_in, opp_in, near_in,
    bc_part, b_out, b_in, b_full, pay, pay_in, q_out, q_in, q_own, q_full,
    x_send, x_recv, s_send, s_recv, wx_sem, e_sem, m_sem,
    core_sem, y_send, y_recv, low_sem, g_send, g_recv,
    dx_send, dx_recv, part_send, part_recv, opp_send, opp_recv, near_send, near_recv,
    bs_sem, br_sem, cs_sem, cr_sem,
    ys_sem, yr_sem, qs_sem, qr_sem, hs_sem, hr_sem,
):
    me = lax.axis_index("tensor")
    z = me // 2
    xl = me % 2
    zp = ((z + 1) % 4) * 2 + xl
    zm = ((z + 3) % 4) * 2 + xl
    zo = ((z + 2) % 4) * 2 + xl
    xp = z * 2 + (1 - xl)

    w = lax.axis_index("dp")
    core = w % 2
    xh = (w // 2) % 2
    y = w // 4
    other_core = w + 1 - 2 * core
    other_x = w + 2 - 4 * xh

    def y_peer(k):
        return ((y + k) % 4) * 4 + xh * 2 + core

    def loop(count, step_body):
        def step(k, carry):
            step_body(k)
            return carry

        lax.fori_loop(1, count, step, 0)

    barrier = pltpu.get_barrier_semaphore()

    def greet(axis, to):
        pl.semaphore_signal(barrier, inc=1, device_id={axis: to}, device_id_type=MESH)

    loop(NT, lambda k: greet("tensor", (me + k) % NT))
    loop(NDP, lambda k: greet("dp", (w + k) % NDP))

    def wx_copy(b):
        rows = pl.ds(b * CH, CH)
        return pltpu.make_async_copy(wx_hbm.at[rows], wx.at[rows], wx_sem.at[b])

    def e_copy(b):
        rows = pl.ds(b * CH, CH)
        return pltpu.make_async_copy(e_hbm.at[rows], e_all.at[rows], e_sem.at[b])

    for b in range(NT):
        e_copy(b).start()
    for b in range(NT):
        wx_copy(b).start()

    xall[me] = x_ref[...]
    pl.semaphore_wait(barrier, NT - 1 + NDP - 1)

    def x_copy(way, to, src, half):
        part = xall.at[src, pl.ds(half * HALF, HALF)]
        return pltpu.make_async_remote_copy(
            src_ref=part,
            dst_ref=part,
            send_sem=x_send.at[way, src, half],
            recv_sem=x_recv.at[src, half],
            device_id={"tensor": to},
            device_id_type=MESH,
        )

    sent = []

    def send(way, to, src, half):
        copy = x_copy(way, to, src, half)
        copy.start()
        sent.append(copy)

    def arrive(src, half):
        x_copy(0, zp, src, half).wait_recv()

    for half in range(2):
        send(0, zp, me, half)
        send(1, zm, me, half)
        send(2, xp, me, half)

    step = softplus(dt_ref[...])
    rate = head_rates(alog_ref) * step
    upper = (iota((T, T), 0) <= iota((T, T), 1)).astype(F32)
    cum = jnp.dot(rate, upper, precision=HIGH, preferred_element_type=F32)
    cum_ref[...] = cum
    rowp_ref[...] = cum + jnp.log(step)
    keep_bias(doc_ref, bias, bias_t)
    b_part = bc_ref[:, :128]
    c_part = bc_ref[:, 128:]
    scores[...] = dot_nt(c_part, b_part)
    scores_t[...] = dot_nt(b_part, c_part)

    q_hi, q_lo = split2(q_ref[...])
    q_two = jnp.concatenate([q_hi, q_lo], axis=0)

    def e_block(b):
        e_copy(b).wait()
        e_hi, e_lo = split2(e_all[b * CH : (b + 1) * CH])
        both = dot_nt(q_two, e_hi)
        eq_ref[:, b * CH : (b + 1) * CH] = both[:RANK] + both[RANK:] + dot_nt(q_hi, e_lo)

    for b in range(NT):
        e_block(b)

    arrive(zm, 0)
    send(0, zp, zm, 0)
    arrive(xp, 0)
    send(0, zp, xp, 0)
    send(1, zm, xp, 0)

    def weights(h, carry):
        cum_row = cum_ref[pl.ds(h, 1), :]
        rowp_row = rowp_ref[pl.ds(h, 1), :]
        col = to_column(cum_row)
        colp = to_column(rowp_row)
        for i in range(NB):
            here = slice(i * BLK, (i + 1) * BLK)
            for j in range(NB):
                there = slice(j * BLK, (j + 1) * BLK)
                if j <= i:
                    span = rowp_row[:, there] - col[here] + bias[here, there]
                    w_mat[h, here, there] = (scores[here, there] * jnp.exp(span)).astype(BF16)
                if j >= i:
                    span = colp[here] - cum_row[:, there] + bias_t[here, there]
                    wt_mat[h, here, there] = (scores_t[here, there] * jnp.exp(span)).astype(BF16)
        return carry

    lax.fori_loop(0, HEADS, weights, 0)

    arrive(zp, 1)
    send(1, zm, zp, 1)
    arrive(xp, 1)
    send(0, zp, xp, 1)
    send(1, zm, xp, 1)

    for b in range(NT):
        wx_copy(b).wait()
    arrive(zm, 1)
    arrive(zp, 0)

    def product(src):
        rows = pl.ds(pl.multiple_of(src * CH, CH), CH)
        return dot_nn(xall[src], wx[rows, :])

    acc[...] = product(me) + product(xp)
    acc[...] += product(zm) + product(zp)
    arrive(zo, 0)
    send(2, xp, zo, 0)
    arrive(zo, 1)
    send(2, xp, zo, 1)
    acc[...] += product(zo)
    xp_zp = ((z + 1) % 4) * 2 + (1 - xl)
    xp_zm = ((z + 3) % 4) * 2 + (1 - xl)
    xp_zo = ((z + 2) % 4) * 2 + (1 - xl)
    for other in (xp_zp, xp_zm, xp_zo):
        arrive(other, 0)
        arrive(other, 1)
        acc[...] += product(other)
    inner_ref[...] = acc[...].astype(BF16)

    low_lanes = iota((1, BLK), 1) < 64

    def pair_lanes(p):
        return pl.ds(pl.multiple_of(p * BLK, BLK), BLK)

    def pair_skip(p):
        return jnp.where(low_lanes, skip_ref[2 * p], skip_ref[2 * p + 1])

    def gate_parts(lanes):
        gate = gate_ref[:, lanes].astype(F32)
        sig = 1.0 / (1.0 + jnp.exp(-gate))
        return gate, sig, gate * sig

    def mix(p, carry):
        square, product_sum = carry
        lanes = pair_lanes(p)
        x_pair = inner_ref[:, lanes]
        for i in range(NB):
            here = slice(i * BLK, (i + 1) * BLK)
            width = (i + 1) * BLK
            first = dot_nn(w_mat[2 * p, here, :width], x_pair[:width])
            second = dot_nn(w_mat[2 * p + 1, here, :width], x_pair[:width])
            y_buf[here, lanes] = jnp.where(low_lanes, first, second) + pair_skip(
                p
            ) * x_pair[here].astype(F32)
        gate, sig, silu = gate_parts(lanes)
        g = y_buf[:, lanes] * silu
        weighted = dout_ref[:, lanes].astype(F32) * gain_ref[lanes].reshape(1, BLK)
        return square + g * g, product_sum + g * weighted

    zero = jnp.zeros((T, BLK), F32)
    square, product_sum = lax.fori_loop(0, HEADS // 2, mix, (zero, zero))
    sums[0:1, :] = jnp.sum(square.T, axis=0, keepdims=True)
    sums[1:2, :] = jnp.sum(product_sum.T, axis=0, keepdims=True)
    sums[2:8, :] = jnp.zeros((6, T), F32)

    def s_copy(k):
        return pltpu.make_async_remote_copy(
            src_ref=sums,
            dst_ref=sums_in.at[k],
            send_sem=s_send.at[k],
            recv_sem=s_recv.at[k],
            device_id={"tensor": (me + k) % NT},
            device_id_type=MESH,
        )

    for k in range(1, NT):
        s_copy(k).start()
    total = sums[...]
    for k in range(1, NT):
        s_copy(k).wait_recv()
        total = total + sums_in[k]
    r_row = lax.rsqrt(total[0:1] / D + EPSILON)
    r_col = to_column(r_row)
    m_col = to_column(r_row * r_row * r_row * (total[1:2] / D))

    def back(p, carry):
        lanes = pair_lanes(p)
        gate, sig, silu = gate_parts(lanes)
        mixed = y_buf[:, lanes]
        g = mixed * silu
        up = dout_ref[:, lanes].astype(F32)
        dg = r_col * (up * gain_ref[lanes].reshape(1, BLK)) - g * m_col
        dgate_ref[:, lanes] = (dg * mixed * sig * (1.0 + gate * (1.0 - sig))).astype(BF16)
        dy = dg * silu
        dy_low = dy.astype(BF16)
        dy_ref[:, lanes] = dy_low
        pay[pl.ds(p, 1), :] = jnp.sum(up * g * r_col, axis=0, keepdims=True)
        pay[pl.ds(4 + p, 1), :] = jnp.sum(
            dy * inner_ref[:, lanes].astype(F32), axis=0, keepdims=True
        )
        for i in range(NB):
            here = slice(i * BLK, (i + 1) * BLK)
            first = dot_nn(wt_mat[2 * p, here, i * BLK :], dy_low[i * BLK :])
            second = dot_nn(wt_mat[2 * p + 1, here, i * BLK :], dy_low[i * BLK :])
            dxb_ref[here, lanes] = (
                jnp.where(low_lanes, first, second) + pair_skip(p) * dy[here]
            ).astype(BF16)
        return carry

    lax.fori_loop(0, HEADS // 2, back, 0)


    def remote(src, dst, send_sem, recv_sem, axis, to):
        copy = pltpu.make_async_remote_copy(
            src_ref=src, dst_ref=dst, send_sem=send_sem, recv_sem=recv_sem,
            device_id={axis: to}, device_id_type=MESH,
        )
        return copy

    def begin(copy):
        copy.start()
        sent.append(copy)

    dxb = dxb_ref[...]
    q3 = jnp.concatenate(split3(q_ref[...]), axis=0)
    z3 = dot_nt(q3, dxb)
    z_sum = z3[:RANK] + z3[RANK : 2 * RANK] + z3[2 * RANK :]
    z_three = jnp.concatenate(split3(z_sum), axis=0)
    for s in range(NT):
        part = dot_nn(z_three, xall[s])
        part = part[:RANK] + part[RANK : 2 * RANK] + part[2 * RANK :]
        part = part + eq_ref[:, s * CH : (s + 1) * CH]
        p_send[2 * s] = part[:, :256]
        p_send[2 * s + 1] = part[:, 256:]
    core_copy = remote(
        p_send.at[pl.ds((1 - core) * 8, 8)], core_in, core_sem.at[0], core_sem.at[1], "dp",
        other_core,
    )
    begin(core_copy)

    def input_part(s):
        rows = pl.ds(pl.multiple_of(s * CH, CH), CH)
        return dot_nt(dxb, wx[rows, :])

    def dx_copy(i):
        return remote(dx_out.at[i], dx_in.at[i], dx_send.at[i], dx_recv.at[i], "tensor", xp)

    ways = (zp, zm)

    def part_copy(i):
        return remote(
            part_out.at[i], part_in.at[i], part_send.at[i], part_recv.at[i], "tensor", ways[i]
        )

    def opp_copy(i):
        return remote(
            opp_out.at[i], opp_in.at[i], opp_send.at[i], opp_recv.at[i], "tensor", ways[i]
        )

    def near_copy(i, half):
        return remote(
            near_out.at[i, pl.ds(half * HALF, HALF)], near_in.at[i, half],
            near_send.at[i, half], near_recv.at[i, half], "tensor", ways[i],
        )

    dx_out[0] = input_part(xp_zo).astype(BF16)
    begin(dx_copy(0))
    part_out[0] = input_part(xp_zp).astype(BF16)
    begin(part_copy(0))
    part_out[1] = input_part(xp_zm).astype(BF16)
    begin(part_copy(1))

    core_copy.wait_recv()
    for c in range(8):
        p_mid[c] = p_send[core * 8 + c] + core_in[c]

    def y_copy(k):
        to = y_peer(k)
        return remote(
            p_mid.at[pl.ds((to // 4) * 2, 2)], y_in.at[k], y_send.at[k], y_recv.at[k], "dp", to
        )

    for k in range(1, 4):
        begin(y_copy(k))

    to_zp = input_part(zp)
    near_out[0, HALF:] = to_zp[HALF:].astype(BF16)
    near_hold[0] = to_zp[:HALF]
    begin(near_copy(0, 1))
    to_zm = input_part(zm)
    near_out[1, :HALF] = to_zm[:HALF].astype(BF16)
    near_hold[1] = to_zm[HALF:]
    begin(near_copy(1, 0))

    d_scores[...] = jnp.zeros((T, T), F32)

    def head_back(p):
        lanes = slice(p * BLK, (p + 1) * BLK)
        x_pair = inner_ref[:, lanes]
        dy_pair = dy_ref[:, lanes]
        for side in range(2):
            h = 2 * p + side
            mine = low_lanes if side == 0 else jnp.logical_not(low_lanes)
            x_mine = jnp.where(mine, x_pair, jnp.zeros_like(x_pair))
            rowp_row = rowp_ref[h : h + 1, :]
            col = to_column(cum_ref[h : h + 1, :])
            downs = [jnp.zeros((1, BLK), F32) for _ in range(NB)]
            for i in range(NB):
                here = slice(i * BLK, (i + 1) * BLK)
                d_weight = dot_nt(dy_pair[here], x_mine[: (i + 1) * BLK])
                across = jnp.zeros((BLK, BLK), F32)
                for j in range(i + 1):
                    there = slice(j * BLK, (j + 1) * BLK)
                    span = rowp_row[:, there] - col[here] + bias[here, there]
                    d_score = d_weight[:, there] * jnp.exp(span)
                    d_scores[here, there] += d_score
                    both = d_score * scores[here, there]
                    downs[j] = downs[j] + jnp.sum(both, axis=0, keepdims=True)
                    across = across + both
                row_sum[h : h + 1, here] = jnp.sum(across.T, axis=0, keepdims=True)
            for j in range(NB):
                col_sum[h : h + 1, j * BLK : (j + 1) * BLK] = downs[j]

    def m_copy(s):
        rows = pl.ds(s * CH, CH)
        return pltpu.make_async_copy(e_all.at[rows], m_hbm.at[rows], m_sem.at[s])

    def merge(s):
        rows = slice(s * CH, (s + 1) * CH)
        e_all[rows] += lax.dot_general(
            xall[s], dxb_ref[...], (((0,), (0,)), ((), ())), preferred_element_type=F32
        )
        m_copy(s).start()

    head_back(0)
    merge(0)
    for k in range(1, 4):
        y_copy(k).wait_recv()
    for c in range(2):
        p_low[c] = p_mid[y * 2 + c] + y_in[1, c] + y_in[2, c] + y_in[3, c]
    low_copy = remote(p_low.at[1 - xh], x_in, low_sem.at[0], low_sem.at[1], "dp", other_x)
    begin(low_copy)

    head_back(1)
    merge(1)
    low_copy.wait_recv()
    mine = core * 8 + y * 2 + xh
    p_full[mine] = (p_low[xh] + x_in[...]) / NDP

    def g_copy(chunk, to, n):
        return remote(
            p_full.at[chunk], p_full.at[chunk], g_send.at[n], g_recv.at[chunk], "dp", to
        )

    begin(g_copy(mine, other_x, 0))
    for k in range(1, 4):
        begin(g_copy(mine, y_peer(k), k))
    begin(g_copy(mine, other_core, 4))

    dx_copy(0).wait_recv()
    opposite = input_part(zo) + dx_in[0].astype(F32)
    for i in range(2):
        opp_out[i] = opposite[i * HALF : (i + 1) * HALF].astype(BF16)
        begin(opp_copy(i))

    across_x = core * 8 + y * 2 + 1 - xh
    g_copy(across_x, other_x, 0).wait_recv()
    for k in range(1, 4):
        begin(g_copy(across_x, y_peer(k), 4 + k))
    begin(g_copy(across_x, other_core, 8))

    part_copy(0).wait_recv()
    part_copy(1).wait_recv()
    dx_out[1] = (
        input_part(xp) + part_in[0].astype(F32) + part_in[1].astype(F32)
    ).astype(BF16)
    begin(dx_copy(1))

    for k in range(1, 4):
        for c in range(2):
            chunk = core * 8 + ((y + k) % 4) * 2 + c
            g_copy(chunk, other_core, 0).wait_recv()
            begin(g_copy(chunk, other_core, 7 + 2 * k + c))

    head_back(2)
    head_back(3)
    for s in range(2, NT):
        merge(s)

    for i in range(2):
        half = i
        rows = slice(half * HALF, (half + 1) * HALF)
        opp_copy(i).wait_recv()
        near_out[i, rows] = (near_hold[i] + opp_in[i].astype(F32)).astype(BF16)
        begin(near_copy(i, half))

    for c in range(8):
        chunk = (1 - core) * 8 + c
        g_copy(chunk, other_core, 0).wait_recv()

    def gram_add(c, total):
        three = jnp.concatenate(split3(p_full[c]), axis=0)
        return total + dot_nt(three, three)

    g9 = lax.fori_loop(0, NDP, gram_add, jnp.zeros((3 * RANK, 3 * RANK), F32))
    g3 = g9[:RANK] + g9[RANK : 2 * RANK] + g9[2 * RANK :]
    gram = g3[:, :RANK] + g3[:, RANK : 2 * RANK] + g3[:, 2 * RANK :]
    eye = (iota((RANK, RANK), 0) == iota((RANK, RANK), 1)).astype(F32)
    table = jnp.concatenate([eye, gram], axis=1)
    places = iota((RANK, 2 * RANK), 0)
    for j in range(RANK - 1):
        column = table[:, RANK + j : RANK + j + 1]
        row = table[j : j + 1, :]
        pivot = table[j : j + 1, RANK + j : RANK + j + 1]
        table = table - jnp.where(places > j, column * (row / pivot), 0.0)
    pivots = jnp.sum(jnp.where(eye > 0.0, table[:, RANK:], 0.0), axis=1, keepdims=True)
    inverse = table[:, :RANK] * lax.rsqrt(pivots)

    for c in range(NDP):
        ph_ref[:, c * 256 : (c + 1) * 256] = jnp.dot(
            inverse, p_full[c], precision=HIGH, preferred_element_type=F32
        )

    def q_part(s, total):
        lanes = pl.ds(pl.multiple_of(s * CH, CH), CH)
        hi, lo = split2(ph_ref[:, lanes])
        two = jnp.concatenate([hi, lo], axis=0)
        m_hi, m_lo = split2(e_all[lanes, :])
        both = dot_nn(two, m_hi)
        return total + both[:RANK] + both[RANK:] + dot_nn(hi, m_lo)

    q_local = lax.fori_loop(0, NT, q_part, jnp.zeros((RANK, CH), F32))
    for c in range(NDP):
        a, b = c // 4, c % 4
        q_out[c] = q_local[a * 8 : (a + 1) * 8, b * BLK : (b + 1) * BLK]

    def q_copy(k):
        to = (w + k) % NDP
        return remote(q_out.at[to], q_in.at[k], qs_sem.at[k], qr_sem.at[k], "dp", to)

    loop(NDP, lambda k: q_copy(k).start())

    bc_part[:, :128] = dot_nn(d_scores[...].T.astype(BF16), c_part)
    bc_part[:, 128:] = dot_nn(d_scores[...].astype(BF16), b_part)
    rows_each = T // NT
    for s in range(NT):
        b_out[s] = bc_part[s * rows_each : (s + 1) * rows_each].astype(BF16)

    def b_copy(k):
        to = (me + k) % NT
        return remote(b_out.at[to], b_in.at[k], bs_sem.at[k], br_sem.at[k], "tensor", to)

    loop(NT, lambda k: b_copy(k).start())

    lower = (iota((T, T), 0) >= iota((T, T), 1)).astype(F32)
    columns = col_sum[...]
    d_rate = jnp.dot(columns - row_sum[...], lower, precision=HIGH, preferred_element_type=F32)
    raw = dt_ref[...]
    step = softplus(raw)
    decay = head_rates(alog_ref)
    d_step = columns / step + decay * d_rate
    ddt_ref[...] = d_step / (1.0 + jnp.exp(-raw))
    pay[8:16, :] = jnp.broadcast_to(
        jnp.sum(d_rate * decay * step, axis=1, keepdims=True), (HEADS, BLK)
    )
    pay_in[w] = pay[...]

    def pay_copy(k, slot):
        return remote(pay, pay_in.at[slot], ys_sem.at[k], yr_sem.at[k], "dp", (w + k) % NDP)

    loop(NDP, lambda k: pay_copy(k, w).start())

    def q_add(k, total):
        q_copy(k).wait_recv()
        return total + q_in[k]

    q_sum = lax.fori_loop(1, NDP, q_add, q_out[w]) / NDP
    q_own[...] = q_sum
    q_full[w] = q_sum

    def h_copy(k, slot):
        return remote(q_own, q_full.at[slot], hs_sem.at[k], hr_sem.at[k], "dp", (w + k) % NDP)

    loop(NDP, lambda k: h_copy(k, w).start())

    def b_add(k, total):
        b_copy(k).wait_recv()
        return total + b_in[k].astype(F32)

    my_rows = pl.ds(pl.multiple_of(me * rows_each, 16), rows_each)
    b_full[me] = lax.fori_loop(1, NT, b_add, bc_part[my_rows, :]).astype(BF16)

    def c_copy(k, slot):
        return remote(
            b_full.at[slot], b_full.at[slot], cs_sem.at[k], cr_sem.at[k], "tensor", (me + k) % NT
        )

    loop(NT, lambda k: c_copy(k, me).start())

    total = input_part(me)
    for i in range(2):
        for half in range(2):
            near_copy(i, half).wait_recv()
    dx_copy(1).wait_recv()
    for half in range(2):
        rows = slice(half * HALF, (half + 1) * HALF)
        dinp_ref[rows] = (
            total[rows] + near_in[0, half].astype(F32) + near_in[1, half].astype(F32)
            + dx_in[1, rows].astype(F32)
        ).astype(BF16)

    loop(NDP, lambda k: pay_copy(k, (w + NDP - k) % NDP).wait_recv())
    pay_ref[...] = lax.fori_loop(1, NDP, lambda c, t: t + pay_in[c], pay_in[0])
    loop(NT, lambda k: c_copy(k, (me + NT - k) % NT).wait_recv())
    for s in range(NT):
        dbc_ref[s * rows_each : (s + 1) * rows_each] = b_full[s].astype(F32)
    loop(NDP, lambda k: h_copy(k, (w + NDP - k) % NDP).wait_recv())
    for c in range(NDP):
        a, b = c // 4, c % 4
        qm_ref[a * 8 : (a + 1) * 8, b * BLK : (b + 1) * BLK] = q_full[c]

    for copy in sent:
        copy.wait_send()
    for s in range(NT):
        m_copy(s).wait()

    def finish_workers(k):
        pay_copy(k, w).wait_send()
        q_copy(k).wait_send()
        h_copy(k, w).wait_send()

    def finish_shards(k):
        s_copy(k).wait_send()
        b_copy(k).wait_send()
        c_copy(k, me).wait_send()

    loop(NDP, finish_workers)
    loop(NT, finish_shards)


def error_kernel(
    m_ref, ph_ref, qm_ref, dinp_ref, dbc_ref, ddt_ref, dgate_ref, pay_ref,
    out_ref, ph_out, qm_out, dinp_out, dbc_out, ddt_out, dgate_out, gain_out, skip_out, alog_out,
    right,
):
    b = pl.program_id(0)

    @pl.when(b == 0)
    def _():
        q_hi, q_lo = split2(-qm_ref[...])
        right[:RANK] = q_hi
        right[RANK : 2 * RANK] = q_lo
        right[2 * RANK :] = q_hi
        qm_out[...] = qm_ref[...]
        dinp_out[...] = dinp_ref[...]
        dbc_out[...] = dbc_ref[...]
        ddt_out[...] = ddt_ref[...]
        dgate_out[...] = dgate_ref[...]
        for p in range(HEADS // 2):
            gain_out[p * BLK : (p + 1) * BLK] = pay_ref[p]
            skips = pay_ref[4 + p : 5 + p, :]
            skip_out[2 * p] = jnp.sum(skips[:, :64])
            skip_out[2 * p + 1] = jnp.sum(skips[:, 64:])
        for h in range(HEADS):
            alog_out[h] = pay_ref[8 + h, 0]

    ph = ph_ref[...]
    ph_out[...] = ph
    hi, lo = split2(ph)
    left = jnp.concatenate([hi, hi, lo], axis=0)
    out_ref[...] = m_ref[...] + lax.dot_general(
        left, right[...], (((0,), (0,)), ((), ())), preferred_element_type=F32
    )


def vmem():
    return pl.BlockSpec(memory_space=pltpu.VMEM)


def smem():
    return pl.BlockSpec(memory_space=pltpu.SMEM)


def hbm():
    return pl.BlockSpec(memory_space=pl.ANY)


def shape(dims, dtype=F32):
    return jax.ShapeDtypeStruct(dims, dtype)


DMA = pltpu.SemaphoreType.DMA


def shards(
    layer_input, w_x, gate_in, bc, dt_raw, a_log, skip, gain, doc_ids, d_out, q_prev, error_in
):
    merged, ph, qm, d_input, d_bc, d_dt, d_gate, pay = pl.pallas_call(
        main_kernel,
        name="main",
        out_shape=(
            shape((D, CH)), shape((RANK, D)), shape((RANK, CH)), shape((T, CH), BF16),
            shape((T, 256)), shape((HEADS, T)), shape((T, CH), BF16), shape((16, BLK)),
        ),
        in_specs=[vmem(), hbm(), hbm()] + [vmem()] * 4 + [smem(), smem()] + [vmem()] * 3,
        out_specs=(hbm(),) + (vmem(),) * 7,
        scratch_shapes=[
            pltpu.VMEM((NT, T, CH), BF16),
            pltpu.VMEM((D, CH), BF16),
            pltpu.VMEM((D, CH), F32),
            pltpu.VMEM((RANK, D), F32),
            pltpu.VMEM((HEADS, T, T), BF16),
            pltpu.VMEM((HEADS, T, T), BF16),
            pltpu.VMEM((T, T), F32),
            pltpu.VMEM((T, T), F32),
            pltpu.VMEM((T, T), F32),
            pltpu.VMEM((T, T), F32),
            pltpu.VMEM((T, T), F32),
            pltpu.VMEM((HEADS, T), F32),
            pltpu.VMEM((HEADS, T), F32),
            pltpu.VMEM((HEADS, T), F32),
            pltpu.VMEM((HEADS, T), F32),
            pltpu.VMEM((T, CH), F32),
            pltpu.VMEM((T, CH), F32),
            pltpu.VMEM((T, CH), BF16),
            pltpu.VMEM((T, CH), BF16),
            pltpu.VMEM((T, CH), BF16),
            pltpu.VMEM((8, T), F32),
            pltpu.VMEM((NT, 8, T), F32),
            pltpu.VMEM((NDP, RANK, 256), F32),
            pltpu.VMEM((8, RANK, 256), F32),
            pltpu.VMEM((8, RANK, 256), F32),
            pltpu.VMEM((4, 2, RANK, 256), F32),
            pltpu.VMEM((2, RANK, 256), F32),
            pltpu.VMEM((RANK, 256), F32),
            pltpu.VMEM((NDP, RANK, 256), F32),
            pltpu.VMEM((2, T, CH), BF16),
            pltpu.VMEM((2, T, CH), BF16),
            pltpu.VMEM((2, HALF, CH), BF16),
            pltpu.VMEM((2, T, CH), BF16),
            pltpu.VMEM((2, HALF, CH), F32),
            pltpu.VMEM((2, T, CH), BF16),
            pltpu.VMEM((2, T, CH), BF16),
            pltpu.VMEM((2, HALF, CH), BF16),
            pltpu.VMEM((2, 2, HALF, CH), BF16),
            pltpu.VMEM((T, 256), F32),
            pltpu.VMEM((NT, T // NT, 256), BF16),
            pltpu.VMEM((NT, T // NT, 256), BF16),
            pltpu.VMEM((NT, T // NT, 256), BF16),
            pltpu.VMEM((16, BLK), F32),
            pltpu.VMEM((NDP, 16, BLK), F32),
            pltpu.VMEM((NDP, 8, BLK), F32),
            pltpu.VMEM((NDP, 8, BLK), F32),
            pltpu.VMEM((8, BLK), F32),
            pltpu.VMEM((NDP, 8, BLK), F32),
            DMA((3, NT, 2)), DMA((NT, 2)), DMA((NT,)), DMA((NT,)), DMA((NT,)), DMA((NT,)), DMA((NT,)),
            DMA((2,)), DMA((4,)), DMA((4,)), DMA((2,)), DMA((16,)), DMA((NDP,)),
            DMA((2,)), DMA((2,)), DMA((2,)), DMA((2,)), DMA((2,)), DMA((2,)), DMA((2, 2)), DMA((2, 2)),
            DMA((NT,)), DMA((NT,)), DMA((NT,)), DMA((NT,)),
            DMA((NDP,)), DMA((NDP,)), DMA((NDP,)), DMA((NDP,)), DMA((NDP,)), DMA((NDP,)),
        ],
        compiler_params=pltpu.CompilerParams(
            collective_id=0, has_side_effects=True, vmem_limit_bytes=VMEM_LIMIT
        ),
    )(
        layer_input, w_x, error_in, gate_in, d_out, bc, dt_raw, a_log, skip, gain, doc_ids, q_prev,
    )

    def whole(dims):
        return pl.BlockSpec(dims, lambda b: (0,) * len(dims))

    error_out, p_factor, right_mean, d_input, d_bc, d_dt, d_gate, d_gain, d_skip, d_alog = (
        pl.pallas_call(
            error_kernel,
            name="error",
            grid=(NT,),
            out_shape=(
                shape((D, CH)), shape((RANK, D)), shape((RANK, CH)), shape((T, CH), BF16),
                shape((T, 256)), shape((HEADS, T)), shape((T, CH), BF16), shape((CH,)),
                shape((HEADS,)), shape((HEADS,)),
            ),
            in_specs=[
                pl.BlockSpec((CH, CH), lambda b: (b, 0)),
                pl.BlockSpec((RANK, CH), lambda b: (0, b)),
                whole((RANK, CH)),
                whole((T, CH)),
                whole((T, 256)),
                whole((HEADS, T)),
                whole((T, CH)),
                whole((16, BLK)),
            ],
            out_specs=(
                pl.BlockSpec((CH, CH), lambda b: (b, 0)),
                pl.BlockSpec((RANK, CH), lambda b: (0, b)),
                whole((RANK, CH)),
                whole((T, CH)),
                whole((T, 256)),
                whole((HEADS, T)),
                whole((T, CH)),
                whole((CH,)),
                smem(),
                smem(),
            ),
            scratch_shapes=[pltpu.VMEM((3 * RANK, CH), BF16)],
            compiler_params=pltpu.CompilerParams(vmem_limit_bytes=VMEM_LIMIT),
        )(merged, ph, qm, d_input, d_bc, d_dt, d_gate, pay)
    )
    return (
        d_input, d_gate, d_bc, d_dt, d_alog, d_skip, d_gain, p_factor, right_mean, error_out,
    )


def solution(mesh):
    return jax.shard_map(
        shards,
        mesh=mesh,
        in_specs=(
            P("dp", "tensor"),
            P(None, "tensor"),
            P("dp", "tensor"),
            P("dp", None),
            P("tensor", "dp"),
            P("tensor"),
            P("tensor"),
            P("tensor"),
            P("dp"),
            P("dp", "tensor"),
            P(None, "tensor"),
            P("dp", "tensor"),
        ),
        out_specs=(
            P("dp", "tensor"),
            P("dp", "tensor"),
            P("dp", None),
            P("tensor", "dp"),
            P("tensor"),
            P("tensor"),
            P("tensor"),
            P("tensor", None),
            P(None, "tensor"),
            P("dp", "tensor"),
        ),
        check_vma=False,
    )
```

```python
import jax
import jax.numpy as jnp
from jax import lax
from jax.experimental import pallas as pl
from jax.experimental.pallas import tpu as pltpu
from jax.sharding import PartitionSpec as P

EPSILON = 1e-05
HIGH = lax.Precision.HIGHEST
MESH = pl.DeviceIdType.MESH
F32 = jnp.float32
BF16 = jnp.bfloat16
T = 384
HALF = T // 2
HEADS = 8
CH = 512
NT = 8
NDP = 16
D = 4096
RANK = 32
BLK = 128
NB = T // BLK
LOW = -1e30
MAIN_VMEM = 46 * 1024 * 1024
LAST_VMEM = 20 * 1024 * 1024
ROWS = 1024
FAR = (5, 3, 4, 7, 1, 6, 2)


def dot_nn(a, b):
    return lax.dot_general(a, b, (((1,), (0,)), ((), ())), preferred_element_type=F32)


def dot_nt(a, b):
    return lax.dot_general(a, b, (((1,), (1,)), ((), ())), preferred_element_type=F32)


def split2(v):
    hi = v.astype(BF16)
    lo = (v - hi.astype(F32)).astype(BF16)
    return hi, lo


def split3(v):
    hi = v.astype(BF16)
    rest = v - hi.astype(F32)
    mid = rest.astype(BF16)
    lo = (rest - mid.astype(F32)).astype(BF16)
    return hi, mid, lo


def iota(shape, dim):
    return lax.broadcasted_iota(jnp.int32, shape, dim)


def to_column(row):
    return jnp.broadcast_to(row, (BLK, row.shape[1])).T


def head_rates(alog_ref):
    rows = iota((HEADS, T), 0)
    logs = jnp.zeros((HEADS, T), F32)
    for h in range(HEADS):
        logs = jnp.where(rows == h, alog_ref[h], logs)
    return jnp.exp(logs)


def softplus(v):
    return jnp.maximum(v, 0.0) + jnp.log1p(jnp.exp(-jnp.abs(v)))


def keep_bias(doc_ref, bias_ref, bias_t_ref):
    doc_row = doc_ref[...].astype(F32).reshape(1, T)
    doc_col = to_column(doc_row)
    for i in range(NB):
        for j in range(NB):
            rows = iota((BLK, BLK), 0) + i * BLK
            cols = iota((BLK, BLK), 1) + j * BLK
            same = doc_col[i * BLK : (i + 1) * BLK] == doc_row[:, j * BLK : (j + 1) * BLK]
            spot = (slice(i * BLK, (i + 1) * BLK), slice(j * BLK, (j + 1) * BLK))
            bias_ref[spot] = jnp.where(jnp.logical_and(same, rows >= cols), 0.0, LOW)
            if bias_t_ref is not None:
                bias_t_ref[spot] = jnp.where(jnp.logical_and(same, rows <= cols), 0.0, LOW)


def main_kernel(
    x_hbm, wx_hbm, e_hbm, gate_hbm, dout_hbm, bc_ref, dt_ref, alog_ref, skip_ref, gain_ref,
    doc_ref, q_ref,
    e_all, ph_ref, qm_ref, dinp_ref, dbc_ref, ddt_ref, dgate_ref, pay_ref,
    xall, gate_ref, dout_ref, wx, eq_ref, w_mat, wt_mat, bias, bias_t, scores, scores_t, d_scores,
    cum_ref, rowp_ref, row_sum, col_sum, acc, y_buf, inner_ref, dxb_ref, dy_ref, sums, sums_in,
    p_send, core_in, p_mid, y_in, p_low, x_in, p_full, p_three, grams, m_hi, m_lo,
    dx_out, part_out, opp_out, near_out, near_hold, dx_in, part_in, opp_in, near_in,
    bc_part, b_out, b_in, b_full, pay, pay_in, pay_all, pay_full, q_out, q_in, q_all, q_full,
    x_send, x_recv, s_send, s_recv, wx_sem, e_sem, in_sem,
    core_sem, y_send, y_recv, low_sem, g_send, g_recv,
    dx_send, dx_recv, part_send, part_recv, opp_send, opp_recv, near_send, near_recv,
    bs_sem, br_sem, cs_sem, cr_sem,
    ys_sem, yr_sem, pay_sem, qs_sem, qr_sem, q_sem,
):
    me = lax.axis_index("tensor")
    z = me // 2
    xl = me % 2
    zp = ((z + 1) % 4) * 2 + xl
    zm = ((z + 3) % 4) * 2 + xl
    zo = ((z + 2) % 4) * 2 + xl
    xp = z * 2 + (1 - xl)

    w = lax.axis_index("dp")
    core = w % 2
    xh = (w // 2) % 2
    y = w // 4
    other_core = w + 1 - 2 * core
    place = y * 2 + xh
    other_x = w + 2 - 4 * xh

    def y_peer(k):
        return ((y + k) % 4) * 4 + xh * 2 + core

    def same_core(k):
        return ((place + k) % 8) * 2 + core

    def loop(count, step_body):
        def step(k, carry):
            step_body(k)
            return carry

        lax.fori_loop(1, count, step, 0)

    barrier = pltpu.get_barrier_semaphore()

    def greet(axis, to):
        pl.semaphore_signal(barrier, inc=1, device_id={axis: to}, device_id_type=MESH)

    loop(NT, lambda k: greet("tensor", (me + k) % NT))
    loop(NDP, lambda k: greet("dp", (w + k) % NDP))

    def wx_copy(b):
        rows = pl.ds(b * CH, CH)
        return pltpu.make_async_copy(wx_hbm.at[rows], wx.at[rows], wx_sem.at[b])

    def e_copy(b):
        rows = pl.ds(b * CH, CH)
        return pltpu.make_async_copy(e_hbm.at[rows], e_all.at[rows], e_sem.at[b])

    own_load = pltpu.make_async_copy(x_hbm, xall.at[me], in_sem.at[0])
    gate_load = pltpu.make_async_copy(gate_hbm, gate_ref, in_sem.at[1])
    dout_load = pltpu.make_async_copy(dout_hbm, dout_ref, in_sem.at[2])
    own_load.start()
    for b in range(NT):
        e_copy(b).start()
    for b in range(NT):
        wx_copy(b).start()
    gate_load.start()
    dout_load.start()
    pl.semaphore_wait(barrier, NT - 1 + NDP - 1)

    def x_copy(way, to, src, half):
        part = xall.at[src, pl.ds(half * HALF, HALF)]
        return pltpu.make_async_remote_copy(
            src_ref=part,
            dst_ref=part,
            send_sem=x_send.at[way, src, half],
            recv_sem=x_recv.at[src, half],
            device_id={"tensor": to},
            device_id_type=MESH,
        )

    sent = []

    def send(way, to, src, half):
        copy = x_copy(way, to, src, half)
        copy.start()
        sent.append(copy)

    def send_own(way, to, half):
        rows = pl.ds(half * HALF, HALF)
        copy = pltpu.make_async_remote_copy(
            src_ref=x_hbm.at[rows],
            dst_ref=xall.at[me, rows],
            send_sem=x_send.at[way, me, half],
            recv_sem=x_recv.at[me, half],
            device_id={"tensor": to},
            device_id_type=MESH,
        )
        copy.start()
        sent.append(copy)

    def arrive(src, half):
        x_copy(0, zp, src, half).wait_recv()

    for half in range(2):
        send_own(0, zp, half)
        send_own(1, zm, 1 - half)
        send_own(2, xp, half)

    step = softplus(dt_ref[...])
    rate = head_rates(alog_ref) * step
    upper = (iota((T, T), 0) <= iota((T, T), 1)).astype(F32)
    cum = jnp.dot(rate, upper, precision=HIGH, preferred_element_type=F32)
    cum_ref[...] = cum
    rowp_ref[...] = cum + jnp.log(step)
    keep_bias(doc_ref, bias, bias_t)
    b_part = bc_ref[:, :128]
    c_part = bc_ref[:, 128:]
    scores[...] = dot_nt(c_part, b_part)
    scores_t[...] = dot_nt(b_part, c_part)

    q_hi, q_lo = split2(q_ref[...])
    q_two = jnp.concatenate([q_hi, q_lo], axis=0)

    def e_block(b):
        e_copy(b).wait()
        e_hi, e_lo = split2(e_all[b * CH : (b + 1) * CH])
        both = dot_nt(q_two, e_hi)
        eq_ref[:, b * CH : (b + 1) * CH] = both[:RANK] + both[RANK:] + dot_nt(q_hi, e_lo)

    for b in range(5):
        e_block(b)

    arrive(zm, 0)
    send(0, zp, zm, 0)
    arrive(zp, 1)
    send(1, zm, zp, 1)
    arrive(xp, 0)
    send(0, zp, xp, 0)
    send(1, zm, xp, 0)
    for b in range(5, NT):
        e_block(b)

    def weights(h, carry):
        cum_row = cum_ref[pl.ds(h, 1), :]
        rowp_row = rowp_ref[pl.ds(h, 1), :]
        col = to_column(cum_row)
        colp = to_column(rowp_row)
        for i in range(NB):
            here = slice(i * BLK, (i + 1) * BLK)
            for j in range(NB):
                there = slice(j * BLK, (j + 1) * BLK)
                if j <= i:
                    span = rowp_row[:, there] - col[here] + bias[here, there]
                    w_mat[h, here, there] = (scores[here, there] * jnp.exp(span)).astype(BF16)
                if j >= i:
                    span = colp[here] - cum_row[:, there] + bias_t[here, there]
                    wt_mat[h, here, there] = (scores_t[here, there] * jnp.exp(span)).astype(BF16)
        return carry

    lax.fori_loop(0, HEADS, weights, 0)

    arrive(xp, 1)
    send(0, zp, xp, 1)
    send(1, zm, xp, 1)

    for b in range(NT):
        wx_copy(b).wait()
    arrive(zm, 1)
    arrive(zp, 0)

    def product(src):
        rows = pl.ds(pl.multiple_of(src * CH, CH), CH)
        return dot_nn(xall[src], wx[rows, :])

    own_load.wait()
    acc[...] = product(me) + product(xp)
    acc[...] += product(zm) + product(zp)
    arrive(zo, 0)
    send(2, xp, zo, 0)
    arrive(zo, 1)
    send(2, xp, zo, 1)
    acc[...] += product(zo)
    xp_zp = ((z + 1) % 4) * 2 + (1 - xl)
    xp_zm = ((z + 3) % 4) * 2 + (1 - xl)
    xp_zo = ((z + 2) % 4) * 2 + (1 - xl)
    for other in (xp_zp, xp_zm, xp_zo):
        arrive(other, 0)
        arrive(other, 1)
        acc[...] += product(other)
    inner_ref[...] = acc[...].astype(BF16)
    gate_load.wait()
    dout_load.wait()

    low_lanes = iota((1, BLK), 1) < 64

    def pair_lanes(p):
        return pl.ds(pl.multiple_of(p * BLK, BLK), BLK)

    def pair_skip(p):
        return jnp.where(low_lanes, skip_ref[2 * p], skip_ref[2 * p + 1])

    def gate_parts(lanes):
        gate = gate_ref[:, lanes].astype(F32)
        sig = 1.0 / (1.0 + jnp.exp(-gate))
        return gate, sig, gate * sig

    def mix(p, carry):
        square, product_sum = carry
        lanes = pair_lanes(p)
        x_pair = inner_ref[:, lanes]
        for i in range(NB):
            here = slice(i * BLK, (i + 1) * BLK)
            width = (i + 1) * BLK
            first = dot_nn(w_mat[2 * p, here, :width], x_pair[:width])
            second = dot_nn(w_mat[2 * p + 1, here, :width], x_pair[:width])
            y_buf[here, lanes] = jnp.where(low_lanes, first, second) + pair_skip(
                p
            ) * x_pair[here].astype(F32)
        gate, sig, silu = gate_parts(lanes)
        g = y_buf[:, lanes] * silu
        weighted = dout_ref[:, lanes].astype(F32) * gain_ref[lanes].reshape(1, BLK)
        return square + g * g, product_sum + g * weighted

    zero = jnp.zeros((T, BLK), F32)
    square, product_sum = lax.fori_loop(0, HEADS // 2, mix, (zero, zero))
    sums[0:1, :] = jnp.sum(square.T, axis=0, keepdims=True)
    sums[1:2, :] = jnp.sum(product_sum.T, axis=0, keepdims=True)
    sums[2:8, :] = jnp.zeros((6, T), F32)

    def s_copy(k):
        return pltpu.make_async_remote_copy(
            src_ref=sums,
            dst_ref=sums_in.at[k],
            send_sem=s_send.at[k],
            recv_sem=s_recv.at[k],
            device_id={"tensor": (me + k) % NT},
            device_id_type=MESH,
        )

    for k in range(1, NT):
        s_copy(k).start()
    total = sums[...]
    for k in range(1, NT):
        s_copy(k).wait_recv()
        total = total + sums_in[k]
    r_row = lax.rsqrt(total[0:1] / D + EPSILON)
    r_col = to_column(r_row)
    m_col = to_column(r_row * r_row * r_row * (total[1:2] / D))

    def back(p, carry):
        lanes = pair_lanes(p)
        gate, sig, silu = gate_parts(lanes)
        mixed = y_buf[:, lanes]
        g = mixed * silu
        up = dout_ref[:, lanes].astype(F32)
        dg = r_col * (up * gain_ref[lanes].reshape(1, BLK)) - g * m_col
        dgate_ref[:, lanes] = (dg * mixed * sig * (1.0 + gate * (1.0 - sig))).astype(BF16)
        dy = dg * silu
        dy_low = dy.astype(BF16)
        dy_ref[:, lanes] = dy_low
        pay[pl.ds(p, 1), :] = jnp.sum(up * g * r_col, axis=0, keepdims=True)
        pay[pl.ds(4 + p, 1), :] = jnp.sum(
            dy * inner_ref[:, lanes].astype(F32), axis=0, keepdims=True
        )
        for i in range(NB):
            here = slice(i * BLK, (i + 1) * BLK)
            first = dot_nn(wt_mat[2 * p, here, i * BLK :], dy_low[i * BLK :])
            second = dot_nn(wt_mat[2 * p + 1, here, i * BLK :], dy_low[i * BLK :])
            dxb_ref[here, lanes] = (
                jnp.where(low_lanes, first, second) + pair_skip(p) * dy[here]
            ).astype(BF16)
        return carry

    lax.fori_loop(0, HEADS // 2, back, 0)


    def remote(src, dst, send_sem, recv_sem, axis, to):
        copy = pltpu.make_async_remote_copy(
            src_ref=src, dst_ref=dst, send_sem=send_sem, recv_sem=recv_sem,
            device_id={axis: to}, device_id_type=MESH,
        )
        return copy

    def begin(copy):
        copy.start()
        sent.append(copy)

    dxb = dxb_ref[...]

    def input_part(s):
        rows = pl.ds(pl.multiple_of(s * CH, CH), CH)
        return dot_nt(dxb, wx[rows, :])

    def dx_copy(i):
        return remote(dx_out.at[i], dx_in.at[i], dx_send.at[i], dx_recv.at[i], "tensor", xp)

    ways = (zp, zm)

    def part_copy(i):
        return remote(
            part_out.at[i], part_in.at[i], part_send.at[i], part_recv.at[i], "tensor", ways[i]
        )

    def opp_copy(i):
        return remote(
            opp_out.at[i], opp_in.at[i], opp_send.at[i], opp_recv.at[i], "tensor", ways[i]
        )

    def near_copy(i, half):
        return remote(
            near_out.at[i, pl.ds(half * HALF, HALF)], near_in.at[i, half],
            near_send.at[i, half], near_recv.at[i, half], "tensor", ways[i],
        )

    dx_out[0] = input_part(xp_zo).astype(BF16)
    begin(dx_copy(0))

    q3 = jnp.concatenate(split3(q_ref[...]), axis=0)
    z3 = dot_nt(q3, dxb)
    z_sum = z3[:RANK] + z3[RANK : 2 * RANK] + z3[2 * RANK :]
    z_three = jnp.concatenate(split3(z_sum), axis=0)
    for s in range(NT):
        part = dot_nn(z_three, xall[s])
        part = part[:RANK] + part[RANK : 2 * RANK] + part[2 * RANK :]
        part = part + eq_ref[:, s * CH : (s + 1) * CH]
        p_send[2 * s] = part[:, :256]
        p_send[2 * s + 1] = part[:, 256:]
    core_copy = remote(
        p_send.at[pl.ds((1 - core) * 8, 8)], core_in, core_sem.at[0], core_sem.at[1], "dp",
        other_core,
    )
    begin(core_copy)

    part_out[0] = input_part(xp_zp).astype(BF16)
    begin(part_copy(0))
    part_out[1] = input_part(xp_zm).astype(BF16)
    begin(part_copy(1))

    core_copy.wait_recv()
    for c in range(8):
        p_mid[c] = p_send[core * 8 + c] + core_in[c]

    def y_copy(k):
        to = y_peer(k)
        return remote(
            p_mid.at[pl.ds((to // 4) * 2, 2)], y_in.at[k], y_send.at[k], y_recv.at[k], "dp", to
        )

    for k in (2, 1, 3):
        begin(y_copy(k))

    to_zp = input_part(zp)
    near_out[0, HALF:] = to_zp[HALF:].astype(BF16)
    near_hold[0] = to_zp[:HALF]
    begin(near_copy(0, 1))
    to_zm = input_part(zm)
    near_out[1, :HALF] = to_zm[:HALF].astype(BF16)
    near_hold[1] = to_zm[HALF:]
    begin(near_copy(1, 0))

    d_scores[...] = jnp.zeros((T, T), F32)

    def head_back(p):
        lanes = slice(p * BLK, (p + 1) * BLK)
        x_pair = inner_ref[:, lanes]
        dy_pair = dy_ref[:, lanes]
        for side in range(2):
            h = 2 * p + side
            mine = low_lanes if side == 0 else jnp.logical_not(low_lanes)
            x_mine = jnp.where(mine, x_pair, jnp.zeros_like(x_pair))
            rowp_row = rowp_ref[h : h + 1, :]
            col = to_column(cum_ref[h : h + 1, :])
            downs = [jnp.zeros((1, BLK), F32) for _ in range(NB)]
            for i in range(NB):
                here = slice(i * BLK, (i + 1) * BLK)
                d_weight = dot_nt(dy_pair[here], x_mine[: (i + 1) * BLK])
                across = jnp.zeros((BLK, BLK), F32)
                for j in range(i + 1):
                    there = slice(j * BLK, (j + 1) * BLK)
                    span = rowp_row[:, there] - col[here] + bias[here, there]
                    d_score = d_weight[:, there] * jnp.exp(span)
                    d_scores[here, there] += d_score
                    both = d_score * scores[here, there]
                    downs[j] = downs[j] + jnp.sum(both, axis=0, keepdims=True)
                    across = across + both
                row_sum[h : h + 1, here] = jnp.sum(across.T, axis=0, keepdims=True)
            for j in range(NB):
                col_sum[h : h + 1, j * BLK : (j + 1) * BLK] = downs[j]

    def merge(s):
        rows = slice(s * CH, (s + 1) * CH)
        total = e_all[rows] + lax.dot_general(
            xall[s], dxb_ref[...], (((0,), (0,)), ((), ())), preferred_element_type=F32
        )
        e_all[rows] = total
        hi, lo = split2(total)
        m_hi[rows] = hi
        m_lo[rows] = lo

    head_back(0)
    head_back(1)
    merge(0)
    merge(1)
    for k in range(1, 4):
        y_copy(k).wait_recv()
    for c in range(2):
        p_low[c] = p_mid[y * 2 + c] + y_in[1, c] + y_in[2, c] + y_in[3, c]
    low_copy = remote(p_low.at[1 - xh], x_in, low_sem.at[0], low_sem.at[1], "dp", other_x)
    begin(low_copy)

    dx_copy(0).wait_recv()
    opposite = input_part(zo) + dx_in[0].astype(F32)
    for i in range(2):
        opp_out[i] = opposite[i * HALF : (i + 1) * HALF].astype(BF16)
        begin(opp_copy(i))

    head_back(2)
    mine = core * 8 + place
    low_copy.wait_recv()
    p_full[mine] = (p_low[xh] + x_in[...]) / NDP

    def g_copy(chunk, to, n):
        return remote(
            p_full.at[chunk], p_full.at[chunk], g_send.at[n], g_recv.at[chunk], "dp", to
        )

    begin(g_copy(mine, other_x, 0))
    for k in (2, 1, 3):
        begin(g_copy(mine, y_peer(k), k))
    begin(g_copy(mine, other_core, 4))

    def gram_one(c):
        three = jnp.concatenate(split3(p_full[c]), axis=0)
        p_three[c] = three
        g9 = dot_nt(three, three)
        g3 = g9[:RANK] + g9[RANK : 2 * RANK] + g9[2 * RANK :]
        grams[c] = g3[:, :RANK] + g3[:, RANK : 2 * RANK] + g3[:, 2 * RANK :]

    gram_one(mine)
    head_back(3)

    bc_part[:, :128] = dot_nn(d_scores[...].T.astype(BF16), c_part)
    bc_part[:, 128:] = dot_nn(d_scores[...].astype(BF16), b_part)
    rows_each = T // NT
    for s in range(NT):
        b_out[s] = bc_part[s * rows_each : (s + 1) * rows_each].astype(BF16)

    across_x = core * 8 + y * 2 + 1 - xh
    g_copy(across_x, other_x, 0).wait_recv()
    for k in (2, 1, 3):
        begin(g_copy(across_x, y_peer(k), 4 + k))
    begin(g_copy(across_x, other_core, 8))

    part_copy(0).wait_recv()
    part_copy(1).wait_recv()
    dx_out[1] = (
        input_part(xp) + part_in[0].astype(F32) + part_in[1].astype(F32)
    ).astype(BF16)
    begin(dx_copy(1))
    gram_one(across_x)

    lower = (iota((T, T), 0) >= iota((T, T), 1)).astype(F32)
    columns = col_sum[...]
    d_rate = jnp.dot(columns - row_sum[...], lower, precision=HIGH, preferred_element_type=F32)
    raw = dt_ref[...]
    step = softplus(raw)
    decay = head_rates(alog_ref)
    d_step = columns / step + decay * d_rate
    ddt_ref[...] = d_step / (1.0 + jnp.exp(-raw))
    pay[8:16, :] = jnp.broadcast_to(
        jnp.sum(d_rate * decay * step, axis=1, keepdims=True), (HEADS, BLK)
    )

    pay_core = remote(
        pay.at[pl.ds((1 - core) * 8, 8)], pay_in, pay_sem.at[0], pay_sem.at[1], "dp", other_core
    )
    begin(pay_core)
    for s in range(2, 5):
        merge(s)

    for k in (1, 3, 2):
        for c in range(2):
            chunk = core * 8 + ((y + k) % 4) * 2 + c
            g_copy(chunk, other_core, 0).wait_recv()
            begin(g_copy(chunk, other_core, 7 + 2 * k + c))
            gram_one(chunk)

    pay_core.wait_recv()
    pay_all[place] = pay[pl.ds(core * 8, 8), :] + pay_in[...]

    def pay_copy(k, slot):
        return remote(
            pay_all.at[slot], pay_all.at[slot], ys_sem.at[k], yr_sem.at[k], "dp", same_core(k)
        )

    for k in FAR:
        begin(pay_copy(k, place))

    for i in range(2):
        rows = slice(i * HALF, (i + 1) * HALF)
        opp_copy(i).wait_recv()
        near_out[i, rows] = (near_hold[i] + opp_in[i].astype(F32)).astype(BF16)
        begin(near_copy(i, i))

    def b_copy(k):
        to = (me + k) % NT
        return remote(b_out.at[to], b_in.at[k], bs_sem.at[k], br_sem.at[k], "tensor", to)

    loop(NT, lambda k: b_copy(k).start())
    for s in range(5, NT):
        merge(s)

    for c in range(8):
        chunk = (1 - core) * 8 + c
        g_copy(chunk, other_core, 0).wait_recv()
        gram_one(chunk)

    gram = grams[0]
    for c in range(1, NDP):
        gram = gram + grams[c]
    eye = (iota((RANK, RANK), 0) == iota((RANK, RANK), 1)).astype(F32)
    table = jnp.concatenate([eye, gram], axis=1)
    places = iota((RANK, 2 * RANK), 0)
    for j in range(RANK - 1):
        column = table[:, RANK + j : RANK + j + 1]
        row = table[j : j + 1, :]
        pivot = table[j : j + 1, RANK + j : RANK + j + 1]
        table = table - jnp.where(places > j, column * (row / pivot), 0.0)
    pivots = jnp.sum(jnp.where(eye > 0.0, table[:, RANK:], 0.0), axis=1, keepdims=True)
    inverse = table[:, :RANK] * lax.rsqrt(pivots)

    i_hi, i_mid, i_lo = split3(inverse)
    none = jnp.zeros_like(i_hi)
    left = jnp.concatenate(
        [
            jnp.concatenate([i_hi, i_hi, i_hi], axis=1),
            jnp.concatenate([i_mid, i_mid, none], axis=1),
            jnp.concatenate([i_lo, none, none], axis=1),
        ],
        axis=0,
    )
    q_local = jnp.zeros((RANK, CH), F32)
    for s in range(NT):
        blocks = []
        for c in (2 * s, 2 * s + 1):
            three = dot_nn(left, p_three[c])
            blocks.append(three[:RANK] + three[RANK : 2 * RANK] + three[2 * RANK :])
        ph = jnp.concatenate(blocks, axis=1)
        rows = slice(s * CH, (s + 1) * CH)
        ph_ref[:, rows] = ph
        hi, lo = split2(ph)
        both = dot_nn(jnp.concatenate([hi, lo], axis=0), m_hi[rows])
        q_local = q_local + both[:RANK] + both[RANK:] + dot_nn(hi, m_lo[rows])

    for c in range(2):
        q_out[c] = q_local[c * 16 : (c + 1) * 16]
    q_core = remote(q_out.at[1 - core], q_in, q_sem.at[0], q_sem.at[1], "dp", other_core)
    begin(q_core)
    q_core.wait_recv()
    q_all[place] = q_out[core] + q_in[...]

    def q_copy(k, slot):
        return remote(
            q_all.at[slot], q_all.at[slot], qs_sem.at[k], qr_sem.at[k], "dp", same_core(k)
        )

    for k in FAR:
        begin(q_copy(k, place))

    def b_add(k, total):
        b_copy(k).wait_recv()
        return total + b_in[k].astype(F32)

    my_rows = pl.ds(pl.multiple_of(me * rows_each, 16), rows_each)
    b_full[me] = lax.fori_loop(1, NT, b_add, bc_part[my_rows, :]).astype(BF16)

    def c_copy(k, slot):
        return remote(
            b_full.at[slot], b_full.at[slot], cs_sem.at[k], cr_sem.at[k], "tensor", (me + k) % NT
        )

    loop(NT, lambda k: c_copy(k, me).start())

    total = input_part(me)
    for i in range(2):
        for half in range(2):
            near_copy(i, half).wait_recv()
    dx_copy(1).wait_recv()
    for half in range(2):
        rows = slice(half * HALF, (half + 1) * HALF)
        dinp_ref[rows] = (
            total[rows] + near_in[0, half].astype(F32) + near_in[1, half].astype(F32)
            + dx_in[1, rows].astype(F32)
        ).astype(BF16)

    for k in range(1, 8):
        q_copy(k, (place + 8 - k) % 8).wait_recv()
    q_sum = q_all[0]
    for c in range(1, 8):
        q_sum = q_sum + q_all[c]
    q_full[core] = q_sum / NDP
    q_back = remote(
        q_full.at[core], q_full.at[core], q_sem.at[2], q_sem.at[3], "dp", other_core
    )
    begin(q_back)

    for k in range(1, 8):
        pay_copy(k, (place + 8 - k) % 8).wait_recv()
    pay_sum = pay_all[0]
    for c in range(1, 8):
        pay_sum = pay_sum + pay_all[c]
    pay_full[core] = pay_sum
    pay_back = remote(
        pay_full.at[core], pay_full.at[core], pay_sem.at[2], pay_sem.at[3], "dp", other_core
    )
    begin(pay_back)
    loop(NT, lambda k: c_copy(k, (me + NT - k) % NT).wait_recv())
    for s in range(NT):
        dbc_ref[s * rows_each : (s + 1) * rows_each] = b_full[s].astype(F32)
    remote(
        q_full.at[1 - core], q_full.at[1 - core], q_sem.at[2], q_sem.at[3], "dp", other_core
    ).wait_recv()
    remote(
        pay_full.at[1 - core], pay_full.at[1 - core], pay_sem.at[2], pay_sem.at[3], "dp", other_core
    ).wait_recv()
    for c in range(2):
        pay_ref[c * 8 : (c + 1) * 8] = pay_full[c]
    for c in range(2):
        qm_ref[c * 16 : (c + 1) * 16] = q_full[c]

    for copy in sent:
        copy.wait_send()

    def finish_shards(k):
        s_copy(k).wait_send()
        b_copy(k).wait_send()
        c_copy(k, me).wait_send()

    loop(NT, finish_shards)


def error_kernel(
    m_ref, ph_ref, qm_ref, dinp_ref, dbc_ref, ddt_ref, dgate_ref, pay_ref,
    out_ref, ph_out, qm_out, dinp_out, dbc_out, ddt_out, dgate_out, gain_out, skip_out, alog_out,
    right,
):
    b = pl.program_id(0)

    @pl.when(b == 0)
    def _():
        q_hi, q_lo = split2(-qm_ref[...])
        right[:RANK] = q_hi
        right[RANK : 2 * RANK] = q_lo
        right[2 * RANK :] = q_hi
        qm_out[...] = qm_ref[...]
        dinp_out[...] = dinp_ref[...]
        dbc_out[...] = dbc_ref[...]
        ddt_out[...] = ddt_ref[...]
        dgate_out[...] = dgate_ref[...]
        for p in range(HEADS // 2):
            gain_out[p * BLK : (p + 1) * BLK] = pay_ref[p]
            skips = pay_ref[4 + p : 5 + p, :]
            skip_out[2 * p] = jnp.sum(skips[:, :64])
            skip_out[2 * p + 1] = jnp.sum(skips[:, 64:])
        for h in range(HEADS):
            alog_out[h] = pay_ref[8 + h, 0]

    rows = pl.ds(pl.multiple_of(b * ROWS, ROWS), ROWS)
    ph = ph_ref[:, rows]
    ph_out[...] = ph
    hi, lo = split2(ph)
    left = jnp.concatenate([hi, hi, lo], axis=0)
    out_ref[...] = m_ref[rows, :] + lax.dot_general(
        left, right[...], (((0,), (0,)), ((), ())), preferred_element_type=F32
    )


def vmem():
    return pl.BlockSpec(memory_space=pltpu.VMEM)


def smem():
    return pl.BlockSpec(memory_space=pltpu.SMEM)


def hbm():
    return pl.BlockSpec(memory_space=pl.ANY)


def in_vmem(array):
    return pltpu.with_memory_space_constraint(array, pltpu.VMEM)


def in_hbm(array):
    return pltpu.with_memory_space_constraint(array, pltpu.HBM)


def shape(dims, dtype=F32):
    return jax.ShapeDtypeStruct(dims, dtype)


DMA = pltpu.SemaphoreType.DMA


def shards(
    layer_input, w_x, gate_in, bc, dt_raw, a_log, skip, gain, doc_ids, d_out, q_prev, error_in
):
    merged, ph, qm, d_input, d_bc, d_dt, d_gate, pay = pl.pallas_call(
        main_kernel,
        name="main",
        out_shape=(
            pltpu.VMEM((D, CH), F32), pltpu.VMEM((RANK, D), F32), pltpu.VMEM((RANK, CH), F32),
            pltpu.VMEM((T, CH), BF16), pltpu.VMEM((T, 256), F32), pltpu.VMEM((HEADS, T), F32),
            pltpu.VMEM((T, CH), BF16), pltpu.VMEM((16, BLK), F32),
        ),
        in_specs=[hbm()] * 5 + [vmem()] * 2 + [smem(), smem()] + [vmem()] * 3,
        out_specs=(vmem(),) * 8,
        scratch_shapes=[
            pltpu.VMEM((NT, T, CH), BF16),
            pltpu.VMEM((T, CH), BF16),
            pltpu.VMEM((T, CH), BF16),
            pltpu.VMEM((D, CH), BF16),
            pltpu.VMEM((RANK, D), F32),
            pltpu.VMEM((HEADS, T, T), BF16),
            pltpu.VMEM((HEADS, T, T), BF16),
            pltpu.VMEM((T, T), F32),
            pltpu.VMEM((T, T), F32),
            pltpu.VMEM((T, T), F32),
            pltpu.VMEM((T, T), F32),
            pltpu.VMEM((T, T), F32),
            pltpu.VMEM((HEADS, T), F32),
            pltpu.VMEM((HEADS, T), F32),
            pltpu.VMEM((HEADS, T), F32),
            pltpu.VMEM((HEADS, T), F32),
            pltpu.VMEM((T, CH), F32),
            pltpu.VMEM((T, CH), F32),
            pltpu.VMEM((T, CH), BF16),
            pltpu.VMEM((T, CH), BF16),
            pltpu.VMEM((T, CH), BF16),
            pltpu.VMEM((8, T), F32),
            pltpu.VMEM((NT, 8, T), F32),
            pltpu.VMEM((NDP, RANK, 256), F32),
            pltpu.VMEM((8, RANK, 256), F32),
            pltpu.VMEM((8, RANK, 256), F32),
            pltpu.VMEM((4, 2, RANK, 256), F32),
            pltpu.VMEM((2, RANK, 256), F32),
            pltpu.VMEM((RANK, 256), F32),
            pltpu.VMEM((NDP, RANK, 256), F32),
            pltpu.VMEM((NDP, 3 * RANK, 256), BF16),
            pltpu.VMEM((NDP, RANK, RANK), F32),
            pltpu.VMEM((D, CH), BF16),
            pltpu.VMEM((D, CH), BF16),
            pltpu.VMEM((2, T, CH), BF16),
            pltpu.VMEM((2, T, CH), BF16),
            pltpu.VMEM((2, HALF, CH), BF16),
            pltpu.VMEM((2, T, CH), BF16),
            pltpu.VMEM((2, HALF, CH), F32),
            pltpu.VMEM((2, T, CH), BF16),
            pltpu.VMEM((2, T, CH), BF16),
            pltpu.VMEM((2, HALF, CH), BF16),
            pltpu.VMEM((2, 2, HALF, CH), BF16),
            pltpu.VMEM((T, 256), F32),
            pltpu.VMEM((NT, T // NT, 256), BF16),
            pltpu.VMEM((NT, T // NT, 256), BF16),
            pltpu.VMEM((NT, T // NT, 256), BF16),
            pltpu.VMEM((16, BLK), F32),
            pltpu.VMEM((8, BLK), F32),
            pltpu.VMEM((8, 8, BLK), F32),
            pltpu.VMEM((2, 8, BLK), F32),
            pltpu.VMEM((2, RANK // 2, CH), F32),
            pltpu.VMEM((RANK // 2, CH), F32),
            pltpu.VMEM((8, RANK // 2, CH), F32),
            pltpu.VMEM((2, RANK // 2, CH), F32),
            DMA((3, NT, 2)), DMA((NT, 2)), DMA((NT,)), DMA((NT,)), DMA((NT,)), DMA((NT,)), DMA((3,)),
            DMA((2,)), DMA((4,)), DMA((4,)), DMA((2,)), DMA((16,)), DMA((NDP,)),
            DMA((2,)), DMA((2,)), DMA((2,)), DMA((2,)), DMA((2,)), DMA((2,)), DMA((2, 2)), DMA((2, 2)),
            DMA((NT,)), DMA((NT,)), DMA((NT,)), DMA((NT,)),
            DMA((8,)), DMA((8,)), DMA((4,)), DMA((8,)), DMA((8,)), DMA((4,)),
        ],
        compiler_params=pltpu.CompilerParams(
            collective_id=0, has_side_effects=True, vmem_limit_bytes=MAIN_VMEM
        ),
    )(
        in_hbm(layer_input), in_hbm(w_x), in_hbm(error_in), in_hbm(gate_in), in_hbm(d_out),
        in_hbm(bc), in_hbm(dt_raw), a_log, skip, in_hbm(gain), in_hbm(doc_ids), in_hbm(q_prev),
    )

    def whole(dims):
        return pl.BlockSpec(dims, lambda b: (0,) * len(dims))

    error_out, p_factor, right_mean, d_input, d_bc, d_dt, d_gate, d_gain, d_skip, d_alog = (
        pl.pallas_call(
            error_kernel,
            name="error",
            grid=(D // ROWS,),
            out_shape=(
                shape((D, CH)), shape((RANK, D)), shape((RANK, CH)), shape((T, CH), BF16),
                shape((T, 256)), shape((HEADS, T)), shape((T, CH), BF16), shape((CH,)),
                shape((HEADS,)), shape((HEADS,)),
            ),
            in_specs=[vmem()] * 8,
            out_specs=(
                pl.BlockSpec((ROWS, CH), lambda b: (b, 0)),
                pl.BlockSpec((RANK, ROWS), lambda b: (0, b)),
                whole((RANK, CH)),
                whole((T, CH)),
                whole((T, 256)),
                whole((HEADS, T)),
                whole((T, CH)),
                whole((CH,)),
                smem(),
                smem(),
            ),
            scratch_shapes=[pltpu.VMEM((3 * RANK, CH), BF16)],
            compiler_params=pltpu.CompilerParams(vmem_limit_bytes=LAST_VMEM),
        )(
            in_vmem(merged), in_vmem(ph), in_vmem(qm), in_vmem(d_input), in_vmem(d_bc),
            in_vmem(d_dt), in_vmem(d_gate), in_vmem(pay),
        )
    )
    return (
        d_input, d_gate, d_bc, d_dt, d_alog, d_skip, d_gain, p_factor, right_mean, error_out,
    )


def solution(mesh):
    return jax.shard_map(
        shards,
        mesh=mesh,
        in_specs=(
            P("dp", "tensor"),
            P(None, "tensor"),
            P("dp", "tensor"),
            P("dp", None),
            P("tensor", "dp"),
            P("tensor"),
            P("tensor"),
            P("tensor"),
            P("dp"),
            P("dp", "tensor"),
            P(None, "tensor"),
            P("dp", "tensor"),
        ),
        out_specs=(
            P("dp", "tensor"),
            P("dp", "tensor"),
            P("dp", None),
            P("tensor", "dp"),
            P("tensor"),
            P("tensor"),
            P("tensor"),
            P("tensor", None),
            P(None, "tensor"),
            P("dp", "tensor"),
        ),
        check_vma=False,
    )
```

```python
import jax
import jax.numpy as jnp
from jax import lax
from jax.experimental import pallas as pl
from jax.experimental.pallas import tpu as pltpu
from jax.sharding import PartitionSpec as P

EPSILON = 1e-05
HIGH = lax.Precision.HIGHEST
MESH = pl.DeviceIdType.MESH
F32 = jnp.float32
BF16 = jnp.bfloat16
T = 384
HALF = T // 2
QUARTER = T // 4
HEADS = 8
CH = 512
NT = 8
NDP = 16
D = 4096
RANK = 32
BLK = 128
NB = T // BLK
LOW = -1e30
MAIN_VMEM = 46 * 1024 * 1024
LAST_VMEM = 20 * 1024 * 1024
ROWS = 1024
FAR = (5, 3, 4, 7, 1, 6, 2)


def dot_nn(a, b):
    return lax.dot_general(a, b, (((1,), (0,)), ((), ())), preferred_element_type=F32)


def dot_nt(a, b):
    return lax.dot_general(a, b, (((1,), (1,)), ((), ())), preferred_element_type=F32)


def split2(v):
    hi = v.astype(BF16)
    lo = (v - hi.astype(F32)).astype(BF16)
    return hi, lo


def split3(v):
    hi = v.astype(BF16)
    rest = v - hi.astype(F32)
    mid = rest.astype(BF16)
    lo = (rest - mid.astype(F32)).astype(BF16)
    return hi, mid, lo


def iota(shape, dim):
    return lax.broadcasted_iota(jnp.int32, shape, dim)


def to_column(row):
    return jnp.broadcast_to(row, (BLK, row.shape[1])).T


def head_rates(alog_ref):
    rows = iota((HEADS, T), 0)
    logs = jnp.zeros((HEADS, T), F32)
    for h in range(HEADS):
        logs = jnp.where(rows == h, alog_ref[h], logs)
    return jnp.exp(logs)


def softplus(v):
    return jnp.maximum(v, 0.0) + jnp.log1p(jnp.exp(-jnp.abs(v)))


def keep_bias(doc_ref, bias_ref, bias_t_ref):
    doc_row = doc_ref[...].astype(F32).reshape(1, T)
    doc_col = to_column(doc_row)
    for i in range(NB):
        for j in range(NB):
            rows = iota((BLK, BLK), 0) + i * BLK
            cols = iota((BLK, BLK), 1) + j * BLK
            same = doc_col[i * BLK : (i + 1) * BLK] == doc_row[:, j * BLK : (j + 1) * BLK]
            spot = (slice(i * BLK, (i + 1) * BLK), slice(j * BLK, (j + 1) * BLK))
            bias_ref[spot] = jnp.where(jnp.logical_and(same, rows >= cols), 0.0, LOW)
            if bias_t_ref is not None:
                bias_t_ref[spot] = jnp.where(jnp.logical_and(same, rows <= cols), 0.0, LOW)


def main_kernel(
    x_hbm, wx_hbm, e_hbm, gate_hbm, dout_hbm, bc_ref, dt_ref, alog_ref, skip_ref, gain_ref,
    doc_ref, q_ref,
    e_all, ph_ref, qm_ref, dinp_ref, dbc_ref, ddt_ref, dgate_ref, pay_ref,
    xall, gate_ref, dout_ref, wx, eq_ref, w_mat, wt_mat, bias, bias_t, scores, scores_t, d_scores,
    cum_ref, rowp_ref, row_sum, col_sum, acc, y_buf, inner_ref, dxb_ref, dy_ref, sums, sums_in,
    p_send, core_in, p_mid, y_in, p_low, x_in, p_full, p_three, s_acc, m_hi, m_lo,
    dx_out, part_out, opp_out, near_out, near_hold, dx_in, part_in, opp_in, near_in,
    bc_part, b_out, b_in, b_full, pay, pay_in, pay_all, pay_full, q_out, q_in, q_all, q_full,
    x_send, x_recv, s_send, s_recv, wx_sem, e_sem, in_sem,
    core_sem, y_send, y_recv, low_sem, g_send, g_recv,
    dx_send, dx_recv, part_send, part_recv, opp_send, opp_recv, near_send, near_recv,
    bs_sem, br_sem, cs_sem, cr_sem,
    ys_sem, yr_sem, pay_sem, qs_sem, qr_sem, q_sem,
):
    me = lax.axis_index("tensor")
    z = me // 2
    xl = me % 2
    zp = ((z + 1) % 4) * 2 + xl
    zm = ((z + 3) % 4) * 2 + xl
    zo = ((z + 2) % 4) * 2 + xl
    xp = z * 2 + (1 - xl)

    w = lax.axis_index("dp")
    core = w % 2
    xh = (w // 2) % 2
    y = w // 4
    other_core = w + 1 - 2 * core
    place = y * 2 + xh
    other_x = w + 2 - 4 * xh

    def y_peer(k):
        return ((y + k) % 4) * 4 + xh * 2 + core

    def same_core(k):
        return ((place + k) % 8) * 2 + core

    def loop(count, step_body):
        def step(k, carry):
            step_body(k)
            return carry

        lax.fori_loop(1, count, step, 0)

    barrier = pltpu.get_barrier_semaphore()

    def greet(axis, to):
        pl.semaphore_signal(barrier, inc=1, device_id={axis: to}, device_id_type=MESH)

    loop(NT, lambda k: greet("tensor", (me + k) % NT))
    loop(NDP, lambda k: greet("dp", (w + k) % NDP))

    def wx_copy(b):
        rows = pl.ds(b * CH, CH)
        return pltpu.make_async_copy(wx_hbm.at[rows], wx.at[rows], wx_sem.at[b])

    def e_copy(b):
        rows = pl.ds(b * CH, CH)
        return pltpu.make_async_copy(e_hbm.at[rows], e_all.at[rows], e_sem.at[b])

    own_load = pltpu.make_async_copy(x_hbm, xall.at[me], in_sem.at[0])
    gate_load = pltpu.make_async_copy(gate_hbm, gate_ref, in_sem.at[1])
    dout_load = pltpu.make_async_copy(dout_hbm, dout_ref, in_sem.at[2])
    own_load.start()
    for b in range(NT):
        e_copy(b).start()
    for b in range(NT):
        wx_copy(b).start()
    gate_load.start()
    dout_load.start()
    pl.semaphore_wait(barrier, NT - 1 + NDP - 1)

    def x_copy(way, to, src, part):
        here = xall.at[src, pl.ds(part * QUARTER, QUARTER)]
        return pltpu.make_async_remote_copy(
            src_ref=here,
            dst_ref=here,
            send_sem=x_send.at[way, src, part],
            recv_sem=x_recv.at[src, part],
            device_id={"tensor": to},
            device_id_type=MESH,
        )

    sent = []

    def send(way, to, src, part):
        copy = x_copy(way, to, src, part)
        copy.start()
        sent.append(copy)

    def send_own(way, to, part):
        rows = pl.ds(part * QUARTER, QUARTER)
        copy = pltpu.make_async_remote_copy(
            src_ref=x_hbm.at[rows],
            dst_ref=xall.at[me, rows],
            send_sem=x_send.at[way, me, part],
            recv_sem=x_recv.at[me, part],
            device_id={"tensor": to},
            device_id_type=MESH,
        )
        copy.start()
        sent.append(copy)

    def arrive(src, part):
        x_copy(0, zp, src, part).wait_recv()

    def pass_far(part):
        arrive(zm, part)
        send(0, zp, zm, part)
        arrive(zp, part + 2)
        send(1, zm, zp, part + 2)

    def pass_across(part):
        arrive(xp, part)
        send(0, zp, xp, part)
        send(1, zm, xp, part)

    for part in range(4):
        send_own(0, zp, part)
        send_own(1, zm, (part + 2) % 4)
        send_own(2, xp, part)

    step = softplus(dt_ref[...])
    rate = head_rates(alog_ref) * step
    upper = (iota((T, T), 0) <= iota((T, T), 1)).astype(F32)
    cum = jnp.dot(rate, upper, precision=HIGH, preferred_element_type=F32)
    cum_ref[...] = cum
    rowp_ref[...] = cum + jnp.log(step)
    keep_bias(doc_ref, bias, bias_t)
    b_part = bc_ref[:, :128]
    c_part = bc_ref[:, 128:]
    scores[...] = dot_nt(c_part, b_part)
    scores_t[...] = dot_nt(b_part, c_part)

    q_hi, q_lo = split2(q_ref[...])
    q_two = jnp.concatenate([q_hi, q_lo], axis=0)

    def e_block(b):
        e_copy(b).wait()
        e_hi, e_lo = split2(e_all[b * CH : (b + 1) * CH])
        both = dot_nt(q_two, e_hi)
        eq_ref[:, b * CH : (b + 1) * CH] = both[:RANK] + both[RANK:] + dot_nt(q_hi, e_lo)

    for b in range(3):
        e_block(b)
    pass_far(0)
    for b in range(3, 5):
        e_block(b)
    pass_far(1)
    pass_across(0)
    for b in range(5, NT):
        e_block(b)
    pass_across(1)

    def weights(h, carry):
        cum_row = cum_ref[pl.ds(h, 1), :]
        rowp_row = rowp_ref[pl.ds(h, 1), :]
        col = to_column(cum_row)
        colp = to_column(rowp_row)
        for i in range(NB):
            here = slice(i * BLK, (i + 1) * BLK)
            for j in range(NB):
                there = slice(j * BLK, (j + 1) * BLK)
                if j <= i:
                    span = rowp_row[:, there] - col[here] + bias[here, there]
                    w_mat[h, here, there] = (scores[here, there] * jnp.exp(span)).astype(BF16)
                if j >= i:
                    span = colp[here] - cum_row[:, there] + bias_t[here, there]
                    wt_mat[h, here, there] = (scores_t[here, there] * jnp.exp(span)).astype(BF16)
        return carry

    lax.fori_loop(0, HEADS // 2, weights, 0)
    pass_across(2)
    lax.fori_loop(HEADS // 2, HEADS, weights, 0)
    pass_across(3)

    for b in range(NT):
        wx_copy(b).wait()

    def product(src):
        rows = pl.ds(pl.multiple_of(src * CH, CH), CH)
        return dot_nn(xall[src], wx[rows, :])

    own_load.wait()
    acc[...] = product(me) + product(xp)
    for part in range(2):
        arrive(zo, part)
        send(2, xp, zo, part)
        arrive(zo, part + 2)
        send(2, xp, zo, part + 2)
        if part == 0:
            for half in range(2):
                arrive(zm, half + 2)
                arrive(zp, half)
            acc[...] += product(zm) + product(zp)
    acc[...] += product(zo)
    xp_zp = ((z + 1) % 4) * 2 + (1 - xl)
    xp_zm = ((z + 3) % 4) * 2 + (1 - xl)
    xp_zo = ((z + 2) % 4) * 2 + (1 - xl)
    for other in (xp_zp, xp_zm, xp_zo):
        for part in range(4):
            arrive(other, part)
        acc[...] += product(other)
    inner_ref[...] = acc[...].astype(BF16)
    gate_load.wait()
    dout_load.wait()

    low_lanes = iota((1, BLK), 1) < 64

    def pair_lanes(p):
        return pl.ds(pl.multiple_of(p * BLK, BLK), BLK)

    def pair_skip(p):
        return jnp.where(low_lanes, skip_ref[2 * p], skip_ref[2 * p + 1])

    def gate_parts(lanes):
        gate = gate_ref[:, lanes].astype(F32)
        sig = 1.0 / (1.0 + jnp.exp(-gate))
        return gate, sig, gate * sig

    def mix(p, carry):
        square, product_sum = carry
        lanes = pair_lanes(p)
        x_pair = inner_ref[:, lanes]
        for i in range(NB):
            here = slice(i * BLK, (i + 1) * BLK)
            width = (i + 1) * BLK
            first = dot_nn(w_mat[2 * p, here, :width], x_pair[:width])
            second = dot_nn(w_mat[2 * p + 1, here, :width], x_pair[:width])
            y_buf[here, lanes] = jnp.where(low_lanes, first, second) + pair_skip(
                p
            ) * x_pair[here].astype(F32)
        gate, sig, silu = gate_parts(lanes)
        g = y_buf[:, lanes] * silu
        weighted = dout_ref[:, lanes].astype(F32) * gain_ref[lanes].reshape(1, BLK)
        return square + g * g, product_sum + g * weighted

    zero = jnp.zeros((T, BLK), F32)
    square, product_sum = lax.fori_loop(0, HEADS // 2, mix, (zero, zero))
    sums[0:1, :] = jnp.sum(square.T, axis=0, keepdims=True)
    sums[1:2, :] = jnp.sum(product_sum.T, axis=0, keepdims=True)
    sums[2:8, :] = jnp.zeros((6, T), F32)

    def s_copy(k):
        return pltpu.make_async_remote_copy(
            src_ref=sums,
            dst_ref=sums_in.at[k],
            send_sem=s_send.at[k],
            recv_sem=s_recv.at[k],
            device_id={"tensor": (me + k) % NT},
            device_id_type=MESH,
        )

    for k in range(1, NT):
        s_copy(k).start()
    total = sums[...]
    for k in range(1, NT):
        s_copy(k).wait_recv()
        total = total + sums_in[k]
    r_row = lax.rsqrt(total[0:1] / D + EPSILON)
    r_col = to_column(r_row)
    m_col = to_column(r_row * r_row * r_row * (total[1:2] / D))

    def back(p, carry):
        lanes = pair_lanes(p)
        gate, sig, silu = gate_parts(lanes)
        mixed = y_buf[:, lanes]
        g = mixed * silu
        up = dout_ref[:, lanes].astype(F32)
        dg = r_col * (up * gain_ref[lanes].reshape(1, BLK)) - g * m_col
        dgate_ref[:, lanes] = (dg * mixed * sig * (1.0 + gate * (1.0 - sig))).astype(BF16)
        dy = dg * silu
        dy_low = dy.astype(BF16)
        dy_ref[:, lanes] = dy_low
        pay[pl.ds(p, 1), :] = jnp.sum(up * g * r_col, axis=0, keepdims=True)
        pay[pl.ds(4 + p, 1), :] = jnp.sum(
            dy * inner_ref[:, lanes].astype(F32), axis=0, keepdims=True
        )
        for i in range(NB):
            here = slice(i * BLK, (i + 1) * BLK)
            first = dot_nn(wt_mat[2 * p, here, i * BLK :], dy_low[i * BLK :])
            second = dot_nn(wt_mat[2 * p + 1, here, i * BLK :], dy_low[i * BLK :])
            dxb_ref[here, lanes] = (
                jnp.where(low_lanes, first, second) + pair_skip(p) * dy[here]
            ).astype(BF16)
        return carry

    lax.fori_loop(0, HEADS // 2, back, 0)


    def remote(src, dst, send_sem, recv_sem, axis, to):
        copy = pltpu.make_async_remote_copy(
            src_ref=src, dst_ref=dst, send_sem=send_sem, recv_sem=recv_sem,
            device_id={axis: to}, device_id_type=MESH,
        )
        return copy

    def begin(copy):
        copy.start()
        sent.append(copy)

    dxb = dxb_ref[...]

    def input_part(s):
        rows = pl.ds(pl.multiple_of(s * CH, CH), CH)
        return dot_nt(dxb, wx[rows, :])

    def dx_copy(i):
        return remote(dx_out.at[i], dx_in.at[i], dx_send.at[i], dx_recv.at[i], "tensor", xp)

    ways = (zp, zm)

    def part_copy(i):
        return remote(
            part_out.at[i], part_in.at[i], part_send.at[i], part_recv.at[i], "tensor", ways[i]
        )

    def opp_copy(i):
        return remote(
            opp_out.at[i], opp_in.at[i], opp_send.at[i], opp_recv.at[i], "tensor", ways[i]
        )

    def near_copy(i, half):
        return remote(
            near_out.at[i, pl.ds(half * HALF, HALF)], near_in.at[i, half],
            near_send.at[i, half], near_recv.at[i, half], "tensor", ways[i],
        )

    dx_out[0] = input_part(xp_zo).astype(BF16)
    begin(dx_copy(0))

    q3 = jnp.concatenate(split3(q_ref[...]), axis=0)
    z3 = dot_nt(q3, dxb)
    z_sum = z3[:RANK] + z3[RANK : 2 * RANK] + z3[2 * RANK :]
    z_three = jnp.concatenate(split3(z_sum), axis=0)
    for s in range(NT):
        part = dot_nn(z_three, xall[s])
        part = part[:RANK] + part[RANK : 2 * RANK] + part[2 * RANK :]
        part = part + eq_ref[:, s * CH : (s + 1) * CH]
        p_send[2 * s] = part[:, :256]
        p_send[2 * s + 1] = part[:, 256:]
    core_copy = remote(
        p_send.at[pl.ds((1 - core) * 8, 8)], core_in, core_sem.at[0], core_sem.at[1], "dp",
        other_core,
    )
    begin(core_copy)

    part_out[0] = input_part(xp_zp).astype(BF16)
    begin(part_copy(0))
    part_out[1] = input_part(xp_zm).astype(BF16)
    begin(part_copy(1))

    core_copy.wait_recv()
    for c in range(8):
        p_mid[c] = p_send[core * 8 + c] + core_in[c]

    def y_copy(k):
        to = y_peer(k)
        return remote(
            p_mid.at[pl.ds((to // 4) * 2, 2)], y_in.at[k], y_send.at[k], y_recv.at[k], "dp", to
        )

    for k in (2, 1, 3):
        begin(y_copy(k))

    to_zp = input_part(zp)
    near_out[0, HALF:] = to_zp[HALF:].astype(BF16)
    near_hold[0] = to_zp[:HALF]
    begin(near_copy(0, 1))
    to_zm = input_part(zm)
    near_out[1, :HALF] = to_zm[:HALF].astype(BF16)
    near_hold[1] = to_zm[HALF:]
    begin(near_copy(1, 0))

    d_scores[...] = jnp.zeros((T, T), F32)

    def head_back(p):
        lanes = slice(p * BLK, (p + 1) * BLK)
        x_pair = inner_ref[:, lanes]
        dy_pair = dy_ref[:, lanes]
        for side in range(2):
            h = 2 * p + side
            mine = low_lanes if side == 0 else jnp.logical_not(low_lanes)
            x_mine = jnp.where(mine, x_pair, jnp.zeros_like(x_pair))
            rowp_row = rowp_ref[h : h + 1, :]
            col = to_column(cum_ref[h : h + 1, :])
            downs = [jnp.zeros((1, BLK), F32) for _ in range(NB)]
            for i in range(NB):
                here = slice(i * BLK, (i + 1) * BLK)
                d_weight = dot_nt(dy_pair[here], x_mine[: (i + 1) * BLK])
                across = jnp.zeros((BLK, BLK), F32)
                for j in range(i + 1):
                    there = slice(j * BLK, (j + 1) * BLK)
                    span = rowp_row[:, there] - col[here] + bias[here, there]
                    d_score = d_weight[:, there] * jnp.exp(span)
                    d_scores[here, there] += d_score
                    both = d_score * scores[here, there]
                    downs[j] = downs[j] + jnp.sum(both, axis=0, keepdims=True)
                    across = across + both
                row_sum[h : h + 1, here] = jnp.sum(across.T, axis=0, keepdims=True)
            for j in range(NB):
                col_sum[h : h + 1, j * BLK : (j + 1) * BLK] = downs[j]

    def merge(s):
        rows = slice(s * CH, (s + 1) * CH)
        total = e_all[rows] + lax.dot_general(
            xall[s], dxb_ref[...], (((0,), (0,)), ((), ())), preferred_element_type=F32
        )
        e_all[rows] = total
        hi, lo = split2(total)
        m_hi[rows] = hi
        m_lo[rows] = lo

    head_back(0)
    head_back(1)
    merge(0)
    merge(1)
    merge(2)
    for k in range(1, 4):
        y_copy(k).wait_recv()
    for c in range(2):
        p_low[c] = p_mid[y * 2 + c] + y_in[1, c] + y_in[2, c] + y_in[3, c]
    low_copy = remote(p_low.at[1 - xh], x_in, low_sem.at[0], low_sem.at[1], "dp", other_x)
    begin(low_copy)

    head_back(2)
    merge(3)
    merge(4)
    mine = core * 8 + place
    low_copy.wait_recv()
    p_full[mine] = (p_low[xh] + x_in[...]) / NDP

    def g_copy(chunk, to, n):
        return remote(
            p_full.at[chunk], p_full.at[chunk], g_send.at[n], g_recv.at[chunk], "dp", to
        )

    begin(g_copy(mine, other_x, 0))
    for k in (2, 1, 3):
        begin(g_copy(mine, y_peer(k), k))
    begin(g_copy(mine, other_core, 4))

    dx_copy(0).wait_recv()
    opposite = input_part(zo) + dx_in[0].astype(F32)
    for i in range(2):
        opp_out[i] = opposite[i * HALF : (i + 1) * HALF].astype(BF16)
        begin(opp_copy(i))

    def prepare(c):
        p_three[c] = jnp.concatenate(split3(p_full[c]), axis=0)

    def fold(c):
        rows = pl.ds(pl.multiple_of(c * 256, 256), 256)
        three = p_three[c]
        high = dot_nn(three, m_hi[rows, :])
        low = dot_nn(three[: 2 * RANK], m_lo[rows, :])
        s_acc[...] += (
            high[:RANK] + high[RANK : 2 * RANK] + high[2 * RANK :] + low[:RANK] + low[RANK:]
        )

    prepare(mine)
    head_back(3)
    for s in range(5, NT):
        merge(s)
    s_acc[...] = jnp.zeros((RANK, CH), F32)

    bc_part[:, :128] = dot_nn(d_scores[...].T.astype(BF16), c_part)
    bc_part[:, 128:] = dot_nn(d_scores[...].astype(BF16), b_part)
    rows_each = T // NT
    for s in range(NT):
        b_out[s] = bc_part[s * rows_each : (s + 1) * rows_each].astype(BF16)

    across_x = core * 8 + y * 2 + 1 - xh
    g_copy(across_x, other_x, 0).wait_recv()
    for k in (2, 1, 3):
        begin(g_copy(across_x, y_peer(k), 4 + k))
    begin(g_copy(across_x, other_core, 8))

    part_copy(0).wait_recv()
    part_copy(1).wait_recv()
    dx_out[1] = (
        input_part(xp) + part_in[0].astype(F32) + part_in[1].astype(F32)
    ).astype(BF16)
    begin(dx_copy(1))
    prepare(across_x)
    fold(mine)
    fold(across_x)

    lower = (iota((T, T), 0) >= iota((T, T), 1)).astype(F32)
    columns = col_sum[...]
    d_rate = jnp.dot(columns - row_sum[...], lower, precision=HIGH, preferred_element_type=F32)
    raw = dt_ref[...]
    step = softplus(raw)
    decay = head_rates(alog_ref)
    d_step = columns / step + decay * d_rate
    ddt_ref[...] = d_step / (1.0 + jnp.exp(-raw))
    pay[8:16, :] = jnp.broadcast_to(
        jnp.sum(d_rate * decay * step, axis=1, keepdims=True), (HEADS, BLK)
    )

    pay_core = remote(
        pay.at[pl.ds((1 - core) * 8, 8)], pay_in, pay_sem.at[0], pay_sem.at[1], "dp", other_core
    )
    begin(pay_core)

    def take(chunk):
        g_copy(chunk, other_core, 0).wait_recv()
        prepare(chunk)
        fold(chunk)

    their = (1 - core) * 8
    for c in range(2):
        take(their + y * 2 + c)
    near_chunks = [
        (core * 8 + ((y + k) % 4) * 2 + c, 7 + 2 * k + c) for k in (1, 3, 2) for c in range(2)
    ]
    for chunk, n in near_chunks:
        g_copy(chunk, other_core, 0).wait_recv()
        begin(g_copy(chunk, other_core, n))
    for chunk, n in near_chunks:
        prepare(chunk)
        fold(chunk)
    for i in range(2):
        rows = slice(i * HALF, (i + 1) * HALF)
        opp_copy(i).wait_recv()
        near_out[i, rows] = (near_hold[i] + opp_in[i].astype(F32)).astype(BF16)
        begin(near_copy(i, i))

    for k in (1, 3, 2):
        for c in range(2):
            take(their + ((y + k) % 4) * 2 + c)

    for c in range(2):
        q_out[c] = s_acc[c * 16 : (c + 1) * 16]
    q_core = remote(q_out.at[1 - core], q_in, q_sem.at[0], q_sem.at[1], "dp", other_core)
    begin(q_core)

    def b_copy(k):
        to = (me + k) % NT
        return remote(b_out.at[to], b_in.at[k], bs_sem.at[k], br_sem.at[k], "tensor", to)

    loop(NT, lambda k: b_copy(k).start())

    def gram_add(c, total):
        three = p_three[c]
        return total + dot_nt(three, three)

    g9 = jnp.zeros((3 * RANK, 3 * RANK), F32)
    for c in range(NDP):
        g9 = gram_add(c, g9)
    g3 = g9[:RANK] + g9[RANK : 2 * RANK] + g9[2 * RANK :]
    gram = g3[:, :RANK] + g3[:, RANK : 2 * RANK] + g3[:, 2 * RANK :]

    q_core.wait_recv()
    q_all[place] = q_out[core] + q_in[...]

    def q_copy(k, slot):
        return remote(
            q_all.at[slot], q_all.at[slot], qs_sem.at[k], qr_sem.at[k], "dp", same_core(k)
        )

    for k in FAR:
        begin(q_copy(k, place))

    pay_core.wait_recv()
    pay_all[place] = pay[pl.ds(core * 8, 8), :] + pay_in[...]

    def pay_copy(k, slot):
        return remote(
            pay_all.at[slot], pay_all.at[slot], ys_sem.at[k], yr_sem.at[k], "dp", same_core(k)
        )

    for k in FAR:
        begin(pay_copy(k, place))

    def b_add(k, total):
        b_copy(k).wait_recv()
        return total + b_in[k].astype(F32)

    my_rows = pl.ds(pl.multiple_of(me * rows_each, 16), rows_each)
    b_full[me] = lax.fori_loop(1, NT, b_add, bc_part[my_rows, :]).astype(BF16)

    def c_copy(k, slot):
        return remote(
            b_full.at[slot], b_full.at[slot], cs_sem.at[k], cr_sem.at[k], "tensor", (me + k) % NT
        )

    loop(NT, lambda k: c_copy(k, me).start())

    eye = (iota((RANK, RANK), 0) == iota((RANK, RANK), 1)).astype(F32)
    table = jnp.concatenate([eye, gram], axis=1)
    places = iota((RANK, 2 * RANK), 0)
    for j in range(RANK - 1):
        column = table[:, RANK + j : RANK + j + 1]
        row = table[j : j + 1, :]
        pivot = table[j : j + 1, RANK + j : RANK + j + 1]
        table = table - jnp.where(places > j, column * (row / pivot), 0.0)
    pivots = jnp.sum(jnp.where(eye > 0.0, table[:, RANK:], 0.0), axis=1, keepdims=True)
    inverse = table[:, :RANK] * lax.rsqrt(pivots)

    i_hi, i_mid, i_lo = split3(inverse)
    none = jnp.zeros_like(i_hi)
    left = jnp.concatenate(
        [
            jnp.concatenate([i_hi, i_hi, i_hi], axis=1),
            jnp.concatenate([i_mid, i_mid, none], axis=1),
            jnp.concatenate([i_lo, none, none], axis=1),
        ],
        axis=0,
    )
    for c in range(NDP):
        three = dot_nn(left, p_three[c])
        ph_ref[:, c * 256 : (c + 1) * 256] = (
            three[:RANK] + three[RANK : 2 * RANK] + three[2 * RANK :]
        )

    acc[...] = input_part(me)
    for k in range(1, 8):
        q_copy(k, (place + 8 - k) % 8).wait_recv()
    q_sum = q_all[0]
    for c in range(1, 8):
        q_sum = q_sum + q_all[c]
    q_full[core] = q_sum
    q_back = remote(
        q_full.at[core], q_full.at[core], q_sem.at[2], q_sem.at[3], "dp", other_core
    )
    begin(q_back)

    for i in range(2):
        for half in range(2):
            near_copy(i, half).wait_recv()
    dx_copy(1).wait_recv()
    for half in range(2):
        rows = slice(half * HALF, (half + 1) * HALF)
        dinp_ref[rows] = (
            acc[rows] + near_in[0, half].astype(F32) + near_in[1, half].astype(F32)
            + dx_in[1, rows].astype(F32)
        ).astype(BF16)

    for k in range(1, 8):
        pay_copy(k, (place + 8 - k) % 8).wait_recv()
    pay_sum = pay_all[0]
    for c in range(1, 8):
        pay_sum = pay_sum + pay_all[c]
    pay_full[core] = pay_sum
    pay_back = remote(
        pay_full.at[core], pay_full.at[core], pay_sem.at[2], pay_sem.at[3], "dp", other_core
    )
    begin(pay_back)
    loop(NT, lambda k: c_copy(k, (me + NT - k) % NT).wait_recv())
    for s in range(NT):
        dbc_ref[s * rows_each : (s + 1) * rows_each] = b_full[s].astype(F32)
    remote(
        q_full.at[1 - core], q_full.at[1 - core], q_sem.at[2], q_sem.at[3], "dp", other_core
    ).wait_recv()
    remote(
        pay_full.at[1 - core], pay_full.at[1 - core], pay_sem.at[2], pay_sem.at[3], "dp", other_core
    ).wait_recv()
    for c in range(2):
        pay_ref[c * 8 : (c + 1) * 8] = pay_full[c]
    s_sum = jnp.concatenate([q_full[0], q_full[1]], axis=0)
    qm_ref[...] = (
        jnp.dot(inverse, s_sum, precision=HIGH, preferred_element_type=F32) / NDP
    )

    for copy in sent:
        copy.wait_send()

    def finish_shards(k):
        s_copy(k).wait_send()
        b_copy(k).wait_send()
        c_copy(k, me).wait_send()

    loop(NT, finish_shards)


def error_kernel(
    m_ref, ph_ref, qm_ref, dinp_ref, dbc_ref, ddt_ref, dgate_ref, pay_ref,
    out_ref, ph_out, qm_out, dinp_out, dbc_out, ddt_out, dgate_out, gain_out, skip_out, alog_out,
    right,
):
    b = pl.program_id(0)

    @pl.when(b == 0)
    def _():
        q_hi, q_lo = split2(-qm_ref[...])
        right[:RANK] = q_hi
        right[RANK : 2 * RANK] = q_lo
        right[2 * RANK :] = q_hi
        qm_out[...] = qm_ref[...]
        dinp_out[...] = dinp_ref[...]
        dbc_out[...] = dbc_ref[...]
        ddt_out[...] = ddt_ref[...]
        dgate_out[...] = dgate_ref[...]
        for p in range(HEADS // 2):
            gain_out[p * BLK : (p + 1) * BLK] = pay_ref[p]
            skips = pay_ref[4 + p : 5 + p, :]
            skip_out[2 * p] = jnp.sum(skips[:, :64])
            skip_out[2 * p + 1] = jnp.sum(skips[:, 64:])
        for h in range(HEADS):
            alog_out[h] = pay_ref[8 + h, 0]

    rows = pl.ds(pl.multiple_of(b * ROWS, ROWS), ROWS)
    ph = ph_ref[:, rows]
    ph_out[...] = ph
    hi, lo = split2(ph)
    left = jnp.concatenate([hi, hi, lo], axis=0)
    out_ref[...] = m_ref[rows, :] + lax.dot_general(
        left, right[...], (((0,), (0,)), ((), ())), preferred_element_type=F32
    )


def vmem():
    return pl.BlockSpec(memory_space=pltpu.VMEM)


def smem():
    return pl.BlockSpec(memory_space=pltpu.SMEM)


def hbm():
    return pl.BlockSpec(memory_space=pl.ANY)


def in_vmem(array):
    return pltpu.with_memory_space_constraint(array, pltpu.VMEM)


def in_hbm(array):
    return pltpu.with_memory_space_constraint(array, pltpu.HBM)


def shape(dims, dtype=F32):
    return jax.ShapeDtypeStruct(dims, dtype)


DMA = pltpu.SemaphoreType.DMA


def shards(
    layer_input, w_x, gate_in, bc, dt_raw, a_log, skip, gain, doc_ids, d_out, q_prev, error_in
):
    merged, ph, qm, d_input, d_bc, d_dt, d_gate, pay = pl.pallas_call(
        main_kernel,
        name="main",
        out_shape=(
            pltpu.VMEM((D, CH), F32), pltpu.VMEM((RANK, D), F32), pltpu.VMEM((RANK, CH), F32),
            pltpu.VMEM((T, CH), BF16), pltpu.VMEM((T, 256), F32), pltpu.VMEM((HEADS, T), F32),
            pltpu.VMEM((T, CH), BF16), pltpu.VMEM((16, BLK), F32),
        ),
        in_specs=[hbm()] * 5 + [vmem()] * 2 + [smem(), smem()] + [vmem()] * 3,
        out_specs=(vmem(),) * 8,
        scratch_shapes=[
            pltpu.VMEM((NT, T, CH), BF16),
            pltpu.VMEM((T, CH), BF16),
            pltpu.VMEM((T, CH), BF16),
            pltpu.VMEM((D, CH), BF16),
            pltpu.VMEM((RANK, D), F32),
            pltpu.VMEM((HEADS, T, T), BF16),
            pltpu.VMEM((HEADS, T, T), BF16),
            pltpu.VMEM((T, T), F32),
            pltpu.VMEM((T, T), F32),
            pltpu.VMEM((T, T), F32),
            pltpu.VMEM((T, T), F32),
            pltpu.VMEM((T, T), F32),
            pltpu.VMEM((HEADS, T), F32),
            pltpu.VMEM((HEADS, T), F32),
            pltpu.VMEM((HEADS, T), F32),
            pltpu.VMEM((HEADS, T), F32),
            pltpu.VMEM((T, CH), F32),
            pltpu.VMEM((T, CH), F32),
            pltpu.VMEM((T, CH), BF16),
            pltpu.VMEM((T, CH), BF16),
            pltpu.VMEM((T, CH), BF16),
            pltpu.VMEM((8, T), F32),
            pltpu.VMEM((NT, 8, T), F32),
            pltpu.VMEM((NDP, RANK, 256), F32),
            pltpu.VMEM((8, RANK, 256), F32),
            pltpu.VMEM((8, RANK, 256), F32),
            pltpu.VMEM((4, 2, RANK, 256), F32),
            pltpu.VMEM((2, RANK, 256), F32),
            pltpu.VMEM((RANK, 256), F32),
            pltpu.VMEM((NDP, RANK, 256), F32),
            pltpu.VMEM((NDP, 3 * RANK, 256), BF16),
            pltpu.VMEM((RANK, CH), F32),
            pltpu.VMEM((D, CH), BF16),
            pltpu.VMEM((D, CH), BF16),
            pltpu.VMEM((2, T, CH), BF16),
            pltpu.VMEM((2, T, CH), BF16),
            pltpu.VMEM((2, HALF, CH), BF16),
            pltpu.VMEM((2, T, CH), BF16),
            pltpu.VMEM((2, HALF, CH), F32),
            pltpu.VMEM((2, T, CH), BF16),
            pltpu.VMEM((2, T, CH), BF16),
            pltpu.VMEM((2, HALF, CH), BF16),
            pltpu.VMEM((2, 2, HALF, CH), BF16),
            pltpu.VMEM((T, 256), F32),
            pltpu.VMEM((NT, T // NT, 256), BF16),
            pltpu.VMEM((NT, T // NT, 256), BF16),
            pltpu.VMEM((NT, T // NT, 256), BF16),
            pltpu.VMEM((16, BLK), F32),
            pltpu.VMEM((8, BLK), F32),
            pltpu.VMEM((8, 8, BLK), F32),
            pltpu.VMEM((2, 8, BLK), F32),
            pltpu.VMEM((2, RANK // 2, CH), F32),
            pltpu.VMEM((RANK // 2, CH), F32),
            pltpu.VMEM((8, RANK // 2, CH), F32),
            pltpu.VMEM((2, RANK // 2, CH), F32),
            DMA((3, NT, 4)), DMA((NT, 4)), DMA((NT,)), DMA((NT,)), DMA((NT,)), DMA((NT,)), DMA((3,)),
            DMA((2,)), DMA((4,)), DMA((4,)), DMA((2,)), DMA((16,)), DMA((NDP,)),
            DMA((2,)), DMA((2,)), DMA((2,)), DMA((2,)), DMA((2,)), DMA((2,)), DMA((2, 2)), DMA((2, 2)),
            DMA((NT,)), DMA((NT,)), DMA((NT,)), DMA((NT,)),
            DMA((8,)), DMA((8,)), DMA((4,)), DMA((8,)), DMA((8,)), DMA((4,)),
        ],
        compiler_params=pltpu.CompilerParams(
            collective_id=0, has_side_effects=True, vmem_limit_bytes=MAIN_VMEM
        ),
    )(
        in_hbm(layer_input), in_hbm(w_x), in_hbm(error_in), in_hbm(gate_in), in_hbm(d_out),
        in_hbm(bc), in_hbm(dt_raw), a_log, skip, in_hbm(gain), in_hbm(doc_ids), in_hbm(q_prev),
    )

    def whole(dims):
        return pl.BlockSpec(dims, lambda b: (0,) * len(dims))

    error_out, p_factor, right_mean, d_input, d_bc, d_dt, d_gate, d_gain, d_skip, d_alog = (
        pl.pallas_call(
            error_kernel,
            name="error",
            grid=(D // ROWS,),
            out_shape=(
                shape((D, CH)), shape((RANK, D)), shape((RANK, CH)), shape((T, CH), BF16),
                shape((T, 256)), shape((HEADS, T)), shape((T, CH), BF16), shape((CH,)),
                shape((HEADS,)), shape((HEADS,)),
            ),
            in_specs=[vmem()] * 8,
            out_specs=(
                pl.BlockSpec((ROWS, CH), lambda b: (b, 0)),
                pl.BlockSpec((RANK, ROWS), lambda b: (0, b)),
                whole((RANK, CH)),
                whole((T, CH)),
                whole((T, 256)),
                whole((HEADS, T)),
                whole((T, CH)),
                whole((CH,)),
                smem(),
                smem(),
            ),
            scratch_shapes=[pltpu.VMEM((3 * RANK, CH), BF16)],
            compiler_params=pltpu.CompilerParams(vmem_limit_bytes=LAST_VMEM),
        )(
            in_vmem(merged), in_vmem(ph), in_vmem(qm), in_vmem(d_input), in_vmem(d_bc),
            in_vmem(d_dt), in_vmem(d_gate), in_vmem(pay),
        )
    )
    return (
        d_input, d_gate, d_bc, d_dt, d_alog, d_skip, d_gain, p_factor, right_mean, error_out,
    )


def solution(mesh):
    return jax.shard_map(
        shards,
        mesh=mesh,
        in_specs=(
            P("dp", "tensor"),
            P(None, "tensor"),
            P("dp", "tensor"),
            P("dp", None),
            P("tensor", "dp"),
            P("tensor"),
            P("tensor"),
            P("tensor"),
            P("dp"),
            P("dp", "tensor"),
            P(None, "tensor"),
            P("dp", "tensor"),
        ),
        out_specs=(
            P("dp", "tensor"),
            P("dp", "tensor"),
            P("dp", None),
            P("tensor", "dp"),
            P("tensor"),
            P("tensor"),
            P("tensor"),
            P("tensor", None),
            P(None, "tensor"),
            P("dp", "tensor"),
        ),
        check_vma=False,
    )
```
